128 devices in a mesh: node: 16 (over y, x), local: 8 (over z, core).
Axes of the slice: x: 4, y: 4, z: 4, core: 2. Of those that a mesh axis runs over, the one named last changes fastest.
Arguments:
- inverse: int32 [256, 256], P(('node', 'local')), may hold values from 0 to 1023, as said below
- slot_rows: int32 [16, 8, 16, 8], P('node', 'local'), may hold values from 0 to 1023, as said below
- lengths: int32 [256], P(('node', 'local')), may hold values from 64 to 256
- content: bfloat16 [131072, 1024], P(('node', 'local')), may hold values from -6 to 6
- w_tower: bfloat16 [1024, 1024], replicated, may hold values from -0.1875 to 0.1875
- w_in: bfloat16 [1024, 4096], replicated, may hold values from -0.1875 to 0.1875
- w_out: bfloat16 [1024, 1024], replicated, may hold values from -0.1875 to 0.1875
- out_grad: bfloat16 [256, 256, 1024], P(('node', 'local')), may hold values from -6 to 6
Outputs:
- events_out: bfloat16 [256, 256, 1024], P(('node', 'local'))
- content_grad: bfloat16 [131072, 1024], P(('node', 'local'))
- tower_grad: float32 [1024, 1024], replicated
The draws below stay inside these ranges and needn't reach their ends.
Inputs may be any that keep to these rules, and one draw needn't show every extreme that they name: `inverse`: slots named by events of node n lie in buckets (l, m) whose first slots are named; the 8 slots of one bucket name distinct items, so the events of a node never name two slots of one item; some bucket of every node is full and some owner's buckets are full from every node. `slot_rows`: the 8 rows of one bucket are distinct; slots named by no event hold arbitrary rows.
All inputs are finite; a program needn't handle non-finite values.
Results may differ from the reference program's by a relative error of at most 0.018.
Values may be sent and summed in bfloat16 or wider, within the bound.
No kernel may reach another device: no remote copies, remote signals or barrier semaphores. Data moves between devices by JAX's collectives and lax.ppermute only.
A program may use at most 128 MiB of HBM per device.

```python
import jax
import jax.numpy as jnp
from jax import lax

D = 1024
HEADS = 8
L = 256
CAP = 8
ITEM_DEV = 1024
SEQS = 256
ITEMS = 131072
UNIQ = 1024
N_NODE = 16
N_LOCAL = 8


def draw_inverse(key, part):
    key = jax.random.fold_in(key, 11)
    key_count, key_bucket, key_slot = jax.random.split(key, 3)
    local_ids = jnp.arange(N_LOCAL)[:, None]
    node_ids = jnp.arange(N_NODE)[None, :]
    full_bucket = ((local_ids + node_ids) % 5 == 0) | (local_ids == N_LOCAL - 1) & (node_ids == N_NODE - 1)
    drawn_counts = jax.random.randint(key_count, (N_NODE, N_LOCAL, N_NODE), 1, CAP + 1)
    counts = jnp.where(full_bucket[None], CAP, drawn_counts).reshape(N_NODE, N_LOCAL * N_NODE)
    buckets = jax.random.randint(key_bucket, (SEQS, L), 0, N_LOCAL * N_NODE)
    seq_node = jnp.arange(SEQS) // (SEQS // N_NODE)
    live_count = counts[seq_node[:, None], buckets]
    within = jax.random.randint(key_slot, (SEQS, L), 0, live_count)
    slots = buckets * CAP + within
    position = jnp.arange(L)[None, :]
    slots = jnp.where(position == 0, UNIQ - 1, jnp.where(position == 1, 0, slots))
    return slots.astype(jnp.int32)


def draw_slot_rows(key, part):
    key = jax.random.fold_in(key, 23)
    base = jax.random.randint(key, (N_NODE, N_LOCAL, N_NODE, 1), 0, ITEM_DEV // CAP)
    base = base.at[0, 0, 0, 0].set(ITEM_DEV // CAP - 1)
    base = base.at[N_NODE - 1, N_LOCAL - 1, N_NODE - 1, 0].set(0)
    slot_rows = base * CAP + jnp.arange(CAP)[None, None, None, :]
    return slot_rows.astype(jnp.int32)


def draw_lengths(key, part):
    key = jax.random.fold_in(key, 37)
    drawn = jax.random.randint(key, (SEQS,), L // 4, L + 1)
    index = jnp.arange(SEQS)
    drawn = jnp.where(index % 7 == 0, L, jnp.where(index % 7 == 3, L // 4, drawn))
    return drawn.astype(jnp.int32)


def levels(key, dims, cuts, least, top_value):
    gain = 1.0
    for dim, blocks in cuts:
        draws = jax.random.uniform(jax.random.fold_in(jax.random.fold_in(key, 6), dim), (blocks,), jnp.float32, least / len(cuts), top_value / len(cuts))
        gain = gain * jnp.repeat(jnp.exp(draws), dims[dim] // blocks).reshape((-1,) + (1,) * (len(dims) - 1 - dim))
    return gain


def normal_values(own_key, dims, scale, limit, pieces=(), held_as=jnp.bfloat16):
    loudness = levels(own_key, dims, pieces, -0.22, 0.18) if pieces else 1.0
    result = jax.random.normal(own_key, dims, jnp.float32) * scale * loudness
    return jnp.minimum(jnp.maximum(result, -limit), limit).astype(held_as)


def setup_inputs(seed: int = 0) -> dict:
    seeds = jax.random.split(jax.random.key(seed), 9)
    inverse = draw_inverse(jax.random.fold_in(seeds[8], 71), 0)
    slot_rows = draw_slot_rows(jax.random.fold_in(seeds[8], 71), 0)
    lengths = draw_lengths(jax.random.fold_in(seeds[8], 71), 0)
    content = normal_values(seeds[3], (ITEMS, D), 1.0, 6.0, ((0, 128),))
    w_tower = normal_values(seeds[4], (D, D), D ** -0.5, 0.1875)
    w_in = normal_values(seeds[5], (D, 4 * D), D ** -0.5, 0.1875)
    w_out = normal_values(seeds[6], (D, D), D ** -0.5, 0.1875)
    out_grad = normal_values(seeds[7], (SEQS, L, D), 1.0, 6.0, ((0, 128),))
    return {"inverse": inverse, "slot_rows": slot_rows, "lengths": lengths, "content": content, "w_tower": w_tower, "w_in": w_in, "w_out": w_out, "out_grad": out_grad}


def seq_layer(events, length, w_in, w_out):
    rows, width = events.shape
    head_size = width // HEADS
    normed = (events * lax.rsqrt(lax.optimization_barrier(jnp.mean(events * events, axis=-1, keepdims=True)) + 1e-06)).astype(jnp.bfloat16)
    hidden = jax.nn.silu(jnp.dot(normed, w_in, preferred_element_type=jnp.float32)).astype(jnp.bfloat16)
    gate_part, value_part, query_part, key_part = jnp.split(hidden, 4, axis=1)
    queries = query_part.reshape(rows, HEADS, head_size).astype(jnp.float32)
    keys = key_part.reshape(rows, HEADS, head_size).astype(jnp.float32)
    values = value_part.reshape(rows, HEADS, head_size).astype(jnp.float32)
    scores = jnp.einsum('ihd,jhd->hij', queries, keys) * head_size ** (-0.5)
    position = jnp.arange(rows)
    allowed = (position[None, :] <= position[:, None]) & (position[:, None] < length)
    weights = (jnp.where(allowed[None], jax.nn.silu(scores), 0.0) / length.astype(jnp.float32)).astype(jnp.bfloat16)
    mixed_heads = jnp.einsum('hij,jhd->ihd', weights.astype(jnp.float32), values).reshape(rows, width)
    centred = mixed_heads - lax.optimization_barrier(jnp.mean(mixed_heads, axis=-1, keepdims=True))
    normal = centred * lax.rsqrt(lax.optimization_barrier(jnp.mean(centred * centred, axis=-1, keepdims=True)) + 1e-05)
    gated_rows = (normal * gate_part.astype(jnp.float32)).astype(jnp.bfloat16)
    return events + jnp.dot(gated_rows, w_out, preferred_element_type=jnp.float32)

def silu_slope(values):
    sigma = jax.nn.sigmoid(values)
    return sigma * (1.0 + values * (1.0 - sigma))

def reference(inverse, slot_rows, lengths, content, w_tower, w_in, w_out, out_grad):
    owners = jnp.arange(N_NODE, dtype=jnp.int32)[None, :] * N_LOCAL + jnp.arange(N_LOCAL, dtype=jnp.int32)[:, None]
    item_ids = (owners[None, :, :, None] * ITEM_DEV + slot_rows).reshape(N_NODE * UNIQ).astype(jnp.int32)
    picked = content[item_ids]
    pre_act = jnp.dot(picked, w_tower, preferred_element_type=jnp.float32)
    embedded = jax.nn.silu(pre_act).astype(jnp.bfloat16)
    seq_node = (jnp.arange(SEQS, dtype=jnp.int32) // (SEQS // N_NODE)).astype(jnp.int32)
    flat_slots = (seq_node[:, None] * UNIQ + inverse).astype(jnp.int32)
    events = embedded[flat_slots]

    def one_sequence(packed):
        seq_events, length, cotangent = packed
        layer_out, pullback = jax.vjp(lambda values: seq_layer(values, length, w_in, w_out), seq_events.astype(jnp.float32))
        return (layer_out.astype(jnp.bfloat16), pullback(cotangent.astype(jnp.float32))[0])
    events_out, event_grads = lax.map(one_sequence, (events, lengths, out_grad))
    slot_grads = jnp.zeros((N_NODE * UNIQ, D), jnp.float32).at[flat_slots.reshape(-1)].add(event_grads.reshape(-1, D))
    pre_grads = (slot_grads * silu_slope(pre_act)).astype(jnp.bfloat16)
    row_grads = jnp.dot(pre_grads, w_tower.T, preferred_element_type=jnp.float32)
    content_grad = jnp.zeros((ITEMS, D), jnp.float32).at[item_ids].add(row_grads).astype(jnp.bfloat16)
    tower_grad = jnp.dot(picked.T, pre_grads, preferred_element_type=jnp.float32)
    return (events_out, content_grad, tower_grad)
```

```python
import functools

import jax
import jax.numpy as jnp
from jax import lax
from jax.experimental import pallas as pl
from jax.experimental.pallas import tpu as pltpu
from jax.sharding import PartitionSpec as P

HEADS = 8
BF = jnp.bfloat16
F32 = jnp.float32
NODES = 16
LOCALS = 8
D = 1024
SLOTS = 1024
ROWS = 512
SEQ = 256
MIB = 1 << 20

VMEM = pl.BlockSpec(memory_space=pltpu.VMEM)
SMEM = pl.BlockSpec(memory_space=pltpu.SMEM)
ANY = pl.BlockSpec(memory_space=pl.ANY)


def dot(a, b):
    return jnp.dot(a, b, preferred_element_type=F32)


def dot_nt(a, b):
    return lax.dot_general(a, b, (((1,), (1,)), ((), ())), preferred_element_type=F32)


def dot_tn(a, b):
    return lax.dot_general(a, b, (((0,), (0,)), ((), ())), preferred_element_type=F32)


def sigmoid(v):
    return 0.5 + 0.5 * jnp.tanh(0.5 * v)


def slope_of(v, sigma):
    return sigma * (1.0 + v * (1.0 - sigma))


def pick_kernel(wanted, content, out):
    ids = wanted[...].reshape(128, 128)
    lane = lax.broadcasted_iota(jnp.int32, (128, 128), 1)
    hot = jnp.concatenate(
        [jnp.where(ids == lane + j * 128, 1.0, 0.0).astype(BF) for j in range(8)], axis=1
    )
    out[...] = dot(hot, content[...]).astype(BF).reshape(NODES, 8, D)


def pick(wanted, content):
    return pl.pallas_call(
        pick_kernel,
        out_shape=jax.ShapeDtypeStruct((NODES, 8, D), BF),
        in_specs=[VMEM, VMEM],
        out_specs=VMEM,
        compiler_params=pltpu.CompilerParams(vmem_limit_bytes=12 * MIB),
        cost_estimate=pl.CostEstimate(flops=2 * 128 * D * D, bytes_accessed=3 * MIB, transcendentals=0),
    )(wanted, content)


def layer_kernel(
    pos, lengths, inverse, p0, p1, p2, p3, p4, p5, p6, p7, w_tower_h, w_in_h, w_out_h, grad_h,
    events_out_h, k0, k1, k2, k3, s0, s1, s2, s3,
    table, w_tower, w_in, w_out, grad, out_buf, events, normed, hidden, slope, attn, attn_slope,
    mixed, half, dmixed, dpre, coef, inv_rms, inv_std, hot_gather, hot_scatter,
    sem_p, sem_w, sem_in, sem_out,
):
    me = pos[0]
    pieces = (p0, p1, p2, p3, p4, p5, p6, p7)
    loads = []
    for s, piece in enumerate(pieces):
        at = pl.multiple_of((me ^ s) * 128, 128)
        loads.append(pltpu.make_async_copy(piece, table.at[pl.ds(at, 128)], sem_p.at[s]))
    tower_load = pltpu.make_async_copy(w_tower_h, w_tower, sem_w.at[0])
    out_load = pltpu.make_async_copy(w_out_h, w_out, sem_w.at[1])
    grad_load = pltpu.make_async_copy(grad_h, grad, sem_w.at[2])
    in_loads = [
        pltpu.make_async_copy(
            w_in_h.at[:, pl.ds(j * D, D)], w_in.at[:, pl.ds(j * D, D)], sem_in.at[j]
        )
        for j in range(4)
    ]
    for c in loads:
        c.start()
    tower_load.start()
    for c in in_loads:
        c.start()
    out_load.start()
    grad_load.start()

    for b in range(2):
        row = inverse[b : b + 1, :]
        column = jnp.transpose(jnp.broadcast_to(row, (128, SEQ)))
        lane = lax.broadcasted_iota(jnp.int32, (SEQ, 128), 1)
        sub = lax.broadcasted_iota(jnp.int32, (128, SEQ), 0)
        for j in range(8):
            hot_gather[b * SEQ : (b + 1) * SEQ, j * 128 : (j + 1) * 128] = jnp.where(
                column == lane + j * 128, 1.0, 0.0
            ).astype(BF)
            hot_scatter[j * 128 : (j + 1) * 128, b * SEQ : (b + 1) * SEQ] = jnp.where(
                row == sub + j * 128, 1.0, 0.0
            ).astype(BF)
        length = lengths[b]
        query = lax.broadcasted_iota(jnp.int32, (SEQ, SEQ), 0)
        key = lax.broadcasted_iota(jnp.int32, (SEQ, SEQ), 1)
        share = 1.0 / jnp.full((SEQ, SEQ), length, jnp.int32).astype(F32)
        coef[b] = jnp.where((key <= query) & (query < length), share, 0.0)

    for c in loads:
        c.wait()

    @pl.loop(0, 4)
    def _(c):
        at = pl.ds(pl.multiple_of(c * 256, 256), 256)
        half[:, at] = dot(hot_gather[...], table[:, at]).astype(BF)

    tower_load.wait()

    @pl.loop(0, 4)
    def _(c):
        at = pl.ds(pl.multiple_of(c * 256, 256), 256)
        pre = dot(half[...], w_tower[:, at])
        events[:, at] = (pre * sigmoid(pre)).astype(BF)

    @pl.loop(0, 8)
    def _(i):
        at = pl.ds(pl.multiple_of(i * 64, 64), 64)
        x = events[at, :].astype(F32)
        r = lax.rsqrt(jnp.mean(x * x, axis=-1, keepdims=True) + 1e-06)
        inv_rms[at, :] = jnp.broadcast_to(r, (64, 128))
        normed[at, :] = (x * r).astype(BF)

    for j in range(4):
        in_loads[j].wait()

        @pl.loop(0, 4)
        def _(c):
            at = pl.ds(pl.multiple_of(j * D + c * 256, 256), 256)
            pre = dot(normed[...], w_in[:, at])
            sigma = sigmoid(pre)
            hidden[:, at] = (pre * sigma).astype(BF)
            slope[:, at] = slope_of(pre, sigma).astype(BF)

    scale = 128 ** (-0.5)

    @pl.loop(0, HEADS)
    def _(h):
        for b in range(2):
            rows = slice(b * SEQ, (b + 1) * SEQ)
            head = lambda base: pl.ds(pl.multiple_of(base + h * 128, 128), 128)
            scores = dot_nt(hidden[rows, head(2 * D)], hidden[rows, head(3 * D)]) * scale
            sigma = sigmoid(scores)
            share = coef[b]
            weights = (scores * sigma * share).astype(BF)
            attn[h, b] = weights
            attn_slope[h, b] = (slope_of(scores, sigma) * (share * scale)).astype(BF)
            mixed[rows, head(0)] = dot(weights, hidden[rows, head(D)])

    @pl.loop(0, 8)
    def _(i):
        at = pl.ds(pl.multiple_of(i * 64, 64), 64)
        m = mixed[at, :]
        centred = m - jnp.mean(m, axis=-1, keepdims=True)
        r = lax.rsqrt(jnp.mean(centred * centred, axis=-1, keepdims=True) + 1e-05)
        inv_std[at, :] = jnp.broadcast_to(r, (64, 128))
        normal = centred * r
        mixed[at, :] = normal
        half[at, :] = (normal * hidden[at, 0:D].astype(F32)).astype(BF)

    out_load.wait()
    grad_load.wait()

    @pl.loop(0, 4)
    def _(c):
        at = pl.ds(pl.multiple_of(c * 256, 256), 256)
        out_buf[:, at] = (events[:, at].astype(F32) + dot(half[...], w_out[:, at])).astype(BF)

    store = pltpu.make_async_copy(out_buf, events_out_h, sem_out)
    store.start()

    @pl.loop(0, 4)
    def _(c):
        at = pl.ds(pl.multiple_of(c * 256, 256), 256)
        half[:, at] = dot_nt(grad[...], w_out[at, :]).astype(BF)

    @pl.loop(0, 8)
    def _(i):
        at = pl.ds(pl.multiple_of(i * 64, 64), 64)
        dgated = half[at, :].astype(F32)
        normal = mixed[at, :]
        dgate = (dgated * normal).astype(BF).astype(F32)
        dpre[at, 0:D] = (dgate * slope[at, 0:D].astype(F32)).astype(BF)
        dnormal = dgated * hidden[at, 0:D].astype(F32)
        m1 = jnp.mean(dnormal, axis=-1, keepdims=True)
        m2 = jnp.mean(dnormal * normal, axis=-1, keepdims=True)
        dmixed[at, :] = (inv_std[at, 0:1] * (dnormal - m1 - normal * m2)).astype(BF)

    @pl.loop(0, HEADS)
    def _(h):
        for b in range(2):
            rows = slice(b * SEQ, (b + 1) * SEQ)
            head = lambda base: pl.ds(pl.multiple_of(base + h * 128, 128), 128)
            dm = dmixed[rows, head(0)]
            dw = dot_nt(dm, hidden[rows, head(D)]).astype(BF).astype(F32)
            ds = (dw * attn_slope[h, b].astype(F32)).astype(BF)
            dv = dot_tn(attn[h, b], dm)
            dq = dot(ds, hidden[rows, head(3 * D)])
            dk = dot_tn(ds, hidden[rows, head(2 * D)])
            for base, d in ((D, dv), (2 * D, dq), (3 * D, dk)):
                d = d.astype(BF).astype(F32) * slope[rows, head(base)].astype(F32)
                dpre[rows, head(base)] = d.astype(BF)

    @pl.loop(0, 4)
    def _(c):
        at = pl.ds(pl.multiple_of(c * 256, 256), 256)
        mixed[:, at] = dot_nt(dpre[...], w_in[at, :]).astype(BF).astype(F32)

    @pl.loop(0, 8)
    def _(i):
        at = pl.ds(pl.multiple_of(i * 64, 64), 64)
        dn = mixed[at, :]
        r = inv_rms[at, 0:1]
        unit = events[at, :].astype(F32) * r
        dx = r * (dn - unit * jnp.mean(dn * unit, axis=-1, keepdims=True))
        half[at, :] = (grad[at, :].astype(F32) + dx).astype(BF)

    z, core = me // 2, me % 2
    keeps, sends = (k0, k1, k2, k3), (s0, s1, s2, s3)
    for k in range(4):
        at = pl.ds(pl.multiple_of((z ^ k) * 256, 256), 256)
        got = dot(hot_scatter[...], half[:, at])
        even, odd = got[:, :128], got[:, 128:]
        keeps[k][...] = jnp.where(core == 0, even, odd).astype(BF)
        sends[k][...] = jnp.where(core == 0, odd, even).astype(BF)
    store.wait()


def layer(pos, lengths, inverse, pieces, w_tower, w_in, w_out, out_grad):
    block = jax.ShapeDtypeStruct((SLOTS, 128), BF)
    vm = pltpu.VMEM
    return pl.pallas_call(
        layer_kernel,
        out_shape=[jax.ShapeDtypeStruct((ROWS, D), BF)] + [block] * 8,
        in_specs=[SMEM, SMEM, VMEM] + [ANY] * 12,
        out_specs=[ANY] + [VMEM] * 8,
        scratch_shapes=[
            vm((SLOTS, D), BF), vm((D, D), BF), vm((D, 4 * D), BF), vm((D, D), BF), vm((ROWS, D), BF),
            vm((ROWS, D), BF), vm((ROWS, D), BF), vm((ROWS, D), BF), vm((ROWS, 4 * D), BF),
            vm((ROWS, 4 * D), BF), vm((HEADS, 2, SEQ, SEQ), BF), vm((HEADS, 2, SEQ, SEQ), BF),
            vm((ROWS, D), F32), vm((ROWS, D), BF), vm((ROWS, D), BF), vm((ROWS, 4 * D), BF),
            vm((2, SEQ, SEQ), F32), vm((ROWS, 128), F32), vm((ROWS, 128), F32),
            vm((ROWS, SLOTS), BF), vm((SLOTS, ROWS), BF),
            pltpu.SemaphoreType.DMA((8,)), pltpu.SemaphoreType.DMA((3,)),
            pltpu.SemaphoreType.DMA((4,)), pltpu.SemaphoreType.DMA,
        ],
        compiler_params=pltpu.CompilerParams(vmem_limit_bytes=52 * MIB),
        cost_estimate=pl.CostEstimate(
            flops=14 * 10**9, bytes_accessed=18 * MIB, transcendentals=4 * MIB
        ),
    )(pos, lengths, inverse, *pieces, w_tower, w_in, w_out, out_grad)


def rows_kernel(pos, p0, p1, p2, p3, p4, p5, p6, p7, w_tower_h, turned, slope, w_cols, sem):
    me = pos[0]
    load = pltpu.make_async_copy(
        w_tower_h.at[:, pl.ds(pl.multiple_of(me * 128, 128), 128)], w_cols, sem
    )
    load.start()
    load.wait()
    for s, piece in enumerate((p0, p1, p2, p3, p4, p5, p6, p7)):
        at = pl.ds(pl.multiple_of((me ^ s) * 128, 128), 128)
        rows = piece[...]
        pre = dot(rows, w_cols[...])
        slope[at, :] = slope_of(pre, sigmoid(pre))
        turned[:, at] = jnp.transpose(rows)


def rows_of(pos, pieces, w_tower):
    return pl.pallas_call(
        rows_kernel,
        out_shape=[jax.ShapeDtypeStruct((D, SLOTS), BF), jax.ShapeDtypeStruct((SLOTS, 128), F32)],
        in_specs=[SMEM] + [VMEM] * 8 + [ANY],
        out_specs=[VMEM, VMEM],
        scratch_shapes=[pltpu.VMEM((D, 128), BF), pltpu.SemaphoreType.DMA],
        compiler_params=pltpu.CompilerParams(vmem_limit_bytes=16 * MIB),
        cost_estimate=pl.CostEstimate(
            flops=2 * SLOTS * D * 128, bytes_accessed=5 * MIB, transcendentals=SLOTS * 128
        ),
    )(pos, *pieces, w_tower)


def slots_kernel(a0, a1, a2, a3, slope, turned, out):
    total = a0[...].astype(F32) + a1[...].astype(F32) + a2[...].astype(F32) + a3[...].astype(F32)
    pre = (total * slope[...]).astype(BF)
    tower = dot(turned[...], pre).reshape(NODES, LOCALS, 8, 128)
    for l in range(LOCALS):
        mine = pre[l * 128 : (l + 1) * 128].astype(F32).reshape(NODES, 8, 128)
        both = jnp.concatenate([mine, tower[:, l]], axis=1)
        out[:, l] = both.astype(BF)


def slots(a, slope, turned):
    return pl.pallas_call(
        slots_kernel,
        out_shape=jax.ShapeDtypeStruct((NODES, LOCALS, 16, 128), BF),
        in_specs=[VMEM] * 6,
        out_specs=VMEM,
        compiler_params=pltpu.CompilerParams(vmem_limit_bytes=16 * MIB),
        cost_estimate=pl.CostEstimate(
            flops=2 * SLOTS * D * 128, bytes_accessed=5 * MIB, transcendentals=0
        ),
    )(*a, slope, turned)


def total_kernel(arrived, out):
    acc = arrived[0, :, :, :].astype(F32)
    for n in range(1, NODES):
        acc = acc + arrived[n, :, :, :].astype(F32)
    row = jnp.concatenate([acc[j, 8:, :] for j in range(LOCALS)], axis=1).astype(BF)
    for n in range(NODES):
        out[n] = row


def total(arrived):
    return pl.pallas_call(
        total_kernel,
        out_shape=jax.ShapeDtypeStruct((NODES, 8, D), BF),
        in_specs=[VMEM],
        out_specs=VMEM,
        compiler_params=pltpu.CompilerParams(vmem_limit_bytes=8 * MIB),
        cost_estimate=pl.CostEstimate(flops=MIB, bytes_accessed=MIB, transcendentals=0),
    )(arrived)


def content_kernel(wanted, arrived, w_tower, out, pre):
    for n in range(NODES):
        pre[n * 8 : (n + 1) * 8, :] = jnp.concatenate(
            [arrived[n, j].astype(F32)[:8] for j in range(LOCALS)], axis=1
        )
    rows = dot_nt(pre[...].astype(BF), w_tower[...])
    high = rows.astype(BF)
    low = (rows - high.astype(F32)).astype(BF)
    ids = jnp.transpose(wanted[...].reshape(128, 128))
    sub = lax.broadcasted_iota(jnp.int32, (128, 128), 0)
    for j in range(8):
        hot = jnp.where(ids == sub + j * 128, 1.0, 0.0).astype(BF)
        out[j * 128 : (j + 1) * 128, :] = (dot(hot, high) + dot(hot, low)).astype(BF)


def content_side(wanted, arrived, w_tower):
    return pl.pallas_call(
        content_kernel,
        out_shape=jax.ShapeDtypeStruct((1024, D), BF),
        in_specs=[VMEM] * 3,
        out_specs=VMEM,
        scratch_shapes=[pltpu.VMEM((128, D), F32)],
        compiler_params=pltpu.CompilerParams(vmem_limit_bytes=16 * MIB),
        cost_estimate=pl.CostEstimate(
            flops=6 * 128 * D * D, bytes_accessed=5 * MIB, transcendentals=0
        ),
    )(wanted, arrived, w_tower)


def tower_kernel(pos, p0, p1, p2, p3, p4, p5, p6, p7, out, buf, sem):
    me = pos[0]
    copies = []
    for s, piece in enumerate((p0, p1, p2, p3, p4, p5, p6, p7)):
        buf[s] = piece[...].astype(F32)
        copies.append(pltpu.make_async_copy(buf.at[s], out.at[:, me ^ s], sem.at[s]))
        copies[-1].start()
    for c in copies:
        c.wait()


def tower_side(pos, pieces):
    return pl.pallas_call(
        tower_kernel,
        out_shape=jax.ShapeDtypeStruct((NODES, LOCALS, 8, D), F32),
        in_specs=[SMEM] + [VMEM] * 8,
        out_specs=ANY,
        scratch_shapes=[pltpu.VMEM((8, NODES, 8, D), F32), pltpu.SemaphoreType.DMA((8,))],
        compiler_params=pltpu.CompilerParams(vmem_limit_bytes=16 * MIB),
        cost_estimate=pl.CostEstimate(flops=MIB, bytes_accessed=6 * MIB, transcendentals=0),
    )(pos, *pieces)


def swap(x, s):
    return lax.ppermute(x, "local", [(i, i ^ s) for i in range(LOCALS)])


def gather_local(x):
    got = {0: x}
    for s in (4, 2, 6):
        got[s] = swap(x, s)
    for s in (0, 4, 2, 6):
        got[s + 1] = swap(got[s], 1)
    return [got[s] for s in range(LOCALS)]


def body(inverse, slot_rows, lengths, content, w_tower, w_in, w_out, out_grad):
    pos = lax.axis_index("local").astype(jnp.int32).reshape(1)
    asked = jnp.broadcast_to(slot_rows.reshape(NODES, 8, 1), (NODES, 8, 128))
    wanted = lax.all_to_all(asked, "node", 0, 0, tiled=True)
    picked = pick(wanted, content)
    fetched = lax.all_to_all(picked, "node", 0, 0, tiled=True).reshape(128, D)
    pieces = gather_local(fetched)
    events_out, *blocks = layer(
        pos, lengths, inverse, pieces, w_tower, w_in, w_out, out_grad.reshape(ROWS, D)
    )
    keep, send = blocks[:4], blocks[4:]
    turned, slope = rows_of(pos, pieces, w_tower)
    pair = {k: keep[k] + swap(send[k], 1) for k in (2, 1, 3, 0)}
    arrived = [pair[0]] + [swap(pair[k], 2 * k) for k in (2, 1, 3)]
    out = slots(arrived, slope, turned).reshape(NODES * LOCALS, 16, 128)
    back = lax.all_to_all(out, ("node", "local"), 0, 0, tiled=True).reshape(NODES, LOCALS, 16, 128)
    rows = lax.all_to_all(total(back), "node", 0, 0, tiled=True)
    tower_grad = tower_side(pos, gather_local(rows)).reshape(D, D)
    content_grad = content_side(wanted, back, w_tower)
    return (events_out.reshape(2, SEQ, D), content_grad, tower_grad)


def solution(mesh):
    in_specs = (
        P(("node", "local"), None),
        P("node", "local", None, None),
        P(("node", "local")),
        P(("node", "local"), None),
        P(),
        P(),
        P(),
        P(("node", "local"), None, None),
    )
    out_specs = (P(("node", "local"), None, None), P(("node", "local"), None), P())
    return jax.shard_map(body, mesh=mesh, in_specs=in_specs, out_specs=out_specs, check_vma=False)
```

```python
import functools

import jax
import jax.numpy as jnp
from jax import lax
from jax.experimental import pallas as pl
from jax.experimental.pallas import tpu as pltpu
from jax.sharding import PartitionSpec as P

HEADS = 8
BF = jnp.bfloat16
F32 = jnp.float32
NODES = 16
LOCALS = 8
D = 1024
SLOTS = 1024
ROWS = 512
SEQ = 256
MIB = 1 << 20

VMEM = pl.BlockSpec(memory_space=pltpu.VMEM)
SMEM = pl.BlockSpec(memory_space=pltpu.SMEM)
ANY = pl.BlockSpec(memory_space=pl.ANY)


def dot(a, b):
    return jnp.dot(a, b, preferred_element_type=F32)


def dot_nt(a, b):
    return lax.dot_general(a, b, (((1,), (1,)), ((), ())), preferred_element_type=F32)


def dot_tn(a, b):
    return lax.dot_general(a, b, (((0,), (0,)), ((), ())), preferred_element_type=F32)


def sigmoid(v):
    return 0.5 + 0.5 * jnp.tanh(0.5 * v)


def slope_of(v, sigma):
    return sigma * (1.0 + v * (1.0 - sigma))


def pick_kernel(wanted, content, out):
    ids = wanted[...].reshape(128, 128)
    lane = lax.broadcasted_iota(jnp.int32, (128, 128), 1)
    hot = jnp.concatenate(
        [jnp.where(ids == lane + j * 128, 1.0, 0.0).astype(BF) for j in range(8)], axis=1
    )
    out[...] = dot(hot, content[...]).astype(BF).reshape(NODES, 8, D)


def pick(wanted, content):
    return pl.pallas_call(
        pick_kernel,
        out_shape=jax.ShapeDtypeStruct((NODES, 8, D), BF),
        in_specs=[VMEM, VMEM],
        out_specs=VMEM,
        compiler_params=pltpu.CompilerParams(vmem_limit_bytes=12 * MIB),
        cost_estimate=pl.CostEstimate(flops=2 * 128 * D * D, bytes_accessed=3 * MIB, transcendentals=0),
    )(wanted, content)


def layer_kernel(
    pos, lengths, inverse, p0, p1, p2, p3, p4, p5, p6, p7, w_tower_h, w_in_h, w_out_h, grad_h,
    events_out_h, k0, k1, k2, k3, s0, s1, s2, s3,
    table, w_tower, w_in, w_out, grad, out_buf, events, normed, hidden, slope, attn, attn_slope,
    mixed, half, dgated, dmixed, dpre, coef, inv_rms, inv_std, hot_gather, hot_scatter, pre_a, pre_b,
    sem_w, sem_in, sem_out,
):
    me = pos[0]
    tower_load = pltpu.make_async_copy(w_tower_h, w_tower, sem_w.at[0])
    out_load = pltpu.make_async_copy(w_out_h, w_out, sem_w.at[1])
    grad_load = pltpu.make_async_copy(grad_h, grad, sem_w.at[2])
    in_loads = [
        pltpu.make_async_copy(
            w_in_h.at[:, pl.ds(j * D, D)], w_in.at[:, pl.ds(j * D, D)], sem_in.at[j]
        )
        for j in range(4)
    ]
    tower_load.start()
    for c in in_loads:
        c.start()
    for s, piece in enumerate((p0, p1, p2, p3, p4, p5, p6, p7)):
        table[pl.ds(pl.multiple_of((me ^ s) * 128, 128), 128), :] = piece[...]

    for b in range(2):
        row = inverse[b : b + 1, :]
        column = jnp.transpose(jnp.broadcast_to(row, (128, SEQ)))
        lane = lax.broadcasted_iota(jnp.int32, (SEQ, 128), 1)
        sub = lax.broadcasted_iota(jnp.int32, (128, SEQ), 0)
        for j in range(8):
            hot_gather[b * SEQ : (b + 1) * SEQ, j * 128 : (j + 1) * 128] = jnp.where(
                column == lane + j * 128, 1.0, 0.0
            ).astype(BF)
            hot_scatter[j * 128 : (j + 1) * 128, b * SEQ : (b + 1) * SEQ] = jnp.where(
                row == sub + j * 128, 1.0, 0.0
            ).astype(BF)
        length = lengths[b]
        query = lax.broadcasted_iota(jnp.int32, (SEQ, SEQ), 0)
        key = lax.broadcasted_iota(jnp.int32, (SEQ, SEQ), 1)
        share = (0.5 * 128 ** (-0.5)) / jnp.full((SEQ, SEQ), length, jnp.int32).astype(F32)
        coef[b] = jnp.where((key <= query) & (query < length), share, 0.0)

    @pl.loop(0, 2)
    def _(c):
        at = pl.ds(pl.multiple_of(c * 512, 512), 512)
        half[:, at] = dot(hot_gather[...], table[:, at]).astype(BF)

    tower_load.wait()

    @pl.loop(0, 2)
    def _(c):
        at = pl.ds(pl.multiple_of(c * 512, 512), 512)
        pre = dot(half[...], w_tower[:, at])
        events[:, at] = (pre * sigmoid(pre)).astype(BF)

    out_load.start()
    grad_load.start()

    @pl.loop(0, 8, unroll=2)
    def _(i):
        at = pl.ds(pl.multiple_of(i * 64, 64), 64)
        x = events[at, :].astype(F32)
        r = lax.rsqrt(jnp.mean(x * x, axis=-1, keepdims=True) + 1e-06)
        inv_rms[at, :] = jnp.broadcast_to(r, (64, 128))
        normed[at, :] = (x * r).astype(BF)

    def product(c, into):
        into[...] = dot(normed[...], w_in[:, pl.ds(pl.multiple_of(c * 256, 256), 256)])

    def activate(c, source):
        at = pl.ds(pl.multiple_of(c * 256, 256), 256)
        pre = source[...]
        sigma = sigmoid(pre)
        act = pre * sigma
        hidden[:, at] = act.astype(BF)
        slope[:, at] = (sigma + act * (1.0 - sigma)).astype(BF)

    in_loads[0].wait()
    in_loads[1].wait()
    product(0, pre_a)
    for j in range(2):

        @pl.loop(4 * j, 4 * j + 3 + j)
        def _(i):
            product(2 * i + 1, pre_b)
            activate(2 * i, pre_a)
            product(jnp.minimum(2 * i + 2, 15), pre_a)
            activate(2 * i + 1, pre_b)

        if j == 0:
            in_loads[2].wait()
            in_loads[3].wait()
            product(7, pre_b)
            activate(6, pre_a)
            product(8, pre_a)
            activate(7, pre_b)

    scale = 128 ** (-0.5)
    out_load.wait()
    grad_load.wait()

    @pl.loop(0, HEADS // 2)
    def _(i):
        jobs = [(2 * i + k, b, slice(b * SEQ, (b + 1) * SEQ)) for k in range(2) for b in range(2)]
        head = lambda h, base: pl.ds(pl.multiple_of(base + h * 128, 128), 128)
        score = lambda h, b, rows: dot_nt(
            hidden[rows, head(h, 2 * D)], hidden[rows, head(h, 3 * D)]
        )
        raw = score(*jobs[0])
        for j, (h, b, rows) in enumerate(jobs):
            later = score(*jobs[j + 1]) if j < 3 else None
            turn = jnp.tanh(raw * (0.5 * scale))
            share = coef[b]
            part = share + share * turn
            weights = raw * part
            attn[h, b] = weights.astype(BF)
            rest = (0.5 * scale) - (0.5 * scale) * turn
            attn_slope[h, b] = (part + weights * rest).astype(BF)
            raw = later
        for h, b, rows in jobs:
            mixed[rows, head(h, 0)] = dot(attn[h, b], hidden[rows, head(h, D)])
        at = pl.ds(pl.multiple_of(i * 256, 256), 256)
        dgated[:, at] = dot_nt(grad[...], w_out[at, :]).astype(BF)

    @pl.loop(0, 8, unroll=2)
    def _(i):
        at = pl.ds(pl.multiple_of(i * 64, 64), 64)
        m = mixed[at, :]
        centred = m - jnp.mean(m, axis=-1, keepdims=True)
        r = lax.rsqrt(jnp.mean(centred * centred, axis=-1, keepdims=True) + 1e-05)
        inv_std[at, :] = jnp.broadcast_to(r, (64, 128))
        normal = centred * r
        mixed[at, :] = normal
        half[at, :] = (normal * hidden[at, 0:D].astype(F32)).astype(BF)

    @pl.loop(0, 8, unroll=2)
    def _(i):
        at = pl.ds(pl.multiple_of(i * 64, 64), 64)
        dg = dgated[at, :].astype(F32)
        normal = mixed[at, :]
        dgate = (dg * normal).astype(BF).astype(F32)
        dpre[at, 0:D] = (dgate * slope[at, 0:D].astype(F32)).astype(BF)
        dnormal = dg * hidden[at, 0:D].astype(F32)
        m1 = jnp.mean(dnormal, axis=-1, keepdims=True)
        m2 = jnp.mean(dnormal * normal, axis=-1, keepdims=True)
        dmixed[at, :] = (inv_std[at, 0:1] * (dnormal - m1 - normal * m2)).astype(BF)

    @pl.loop(0, HEADS // 2)
    def _(i):
        jobs = [(2 * i + k, b, slice(b * SEQ, (b + 1) * SEQ)) for k in range(2) for b in range(2)]
        head = lambda h, base: pl.ds(pl.multiple_of(base + h * 128, 128), 128)

        def put(h, rows, base, d):
            d = d.astype(BF).astype(F32) * slope[rows, head(h, base)].astype(F32)
            dpre[rows, head(h, base)] = d.astype(BF)

        dws = [dot_nt(dmixed[rows, head(h, 0)], hidden[rows, head(h, D)]) for h, b, rows in jobs]
        dss = [
            (dw.astype(BF).astype(F32) * attn_slope[h, b].astype(F32)).astype(BF)
            for dw, (h, b, rows) in zip(dws, jobs)
        ]
        for h, b, rows in jobs:
            put(h, rows, D, dot_tn(attn[h, b], dmixed[rows, head(h, 0)]))
        for ds, (h, b, rows) in zip(dss, jobs):
            put(h, rows, 2 * D, dot(ds, hidden[rows, head(h, 3 * D)]))
            put(h, rows, 3 * D, dot_tn(ds, hidden[rows, head(h, 2 * D)]))
        at = pl.ds(pl.multiple_of(i * 256, 256), 256)
        out_buf[:, at] = (events[:, at].astype(F32) + dot(half[...], w_out[:, at])).astype(BF)

    store = pltpu.make_async_copy(out_buf, events_out_h, sem_out)
    store.start()

    @pl.loop(0, 2)
    def _(c):
        at = pl.ds(pl.multiple_of(c * 512, 512), 512)
        mixed[:, at] = dot_nt(dpre[...], w_in[at, :]).astype(BF).astype(F32)

    @pl.loop(0, 8, unroll=2)
    def _(i):
        at = pl.ds(pl.multiple_of(i * 64, 64), 64)
        dn = mixed[at, :]
        r = inv_rms[at, 0:1]
        unit = events[at, :].astype(F32) * r
        dx = r * (dn - unit * jnp.mean(dn * unit, axis=-1, keepdims=True))
        half[at, :] = (grad[at, :].astype(F32) + dx).astype(BF)

    z, core = me // 2, me % 2
    keeps, sends = (k0, k1, k2, k3), (s0, s1, s2, s3)
    for k in range(4):
        at = pl.ds(pl.multiple_of((z ^ k) * 256, 256), 256)
        got = dot(hot_scatter[...], half[:, at])
        even, odd = got[:, :128], got[:, 128:]
        keeps[k][...] = jnp.where(core == 0, even, odd).astype(BF)
        sends[k][...] = jnp.where(core == 0, odd, even).astype(BF)
    store.wait()


def layer(pos, lengths, inverse, pieces, w_tower, w_in, w_out, out_grad):
    block = jax.ShapeDtypeStruct((SLOTS, 128), BF)
    vm = pltpu.VMEM
    return pl.pallas_call(
        layer_kernel,
        out_shape=[jax.ShapeDtypeStruct((ROWS, D), BF)] + [block] * 8,
        in_specs=[SMEM, SMEM] + [VMEM] * 9 + [ANY] * 4,
        out_specs=[ANY] + [VMEM] * 8,
        scratch_shapes=[
            vm((SLOTS, D), BF), vm((D, D), BF), vm((D, 4 * D), BF), vm((D, D), BF), vm((ROWS, D), BF),
            vm((ROWS, D), BF), vm((ROWS, D), BF), vm((ROWS, D), BF), vm((ROWS, 4 * D), BF),
            vm((ROWS, 4 * D), BF), vm((HEADS, 2, SEQ, SEQ), BF), vm((HEADS, 2, SEQ, SEQ), BF),
            vm((ROWS, D), F32), vm((ROWS, D), BF), vm((ROWS, D), BF), vm((ROWS, D), BF), vm((ROWS, 4 * D), BF),
            vm((2, SEQ, SEQ), F32), vm((ROWS, 128), F32), vm((ROWS, 128), F32),
            vm((ROWS, SLOTS), BF), vm((SLOTS, ROWS), BF),
            vm((ROWS, 256), F32), vm((ROWS, 256), F32),
            pltpu.SemaphoreType.DMA((3,)), pltpu.SemaphoreType.DMA((4,)), pltpu.SemaphoreType.DMA,
        ],
        compiler_params=pltpu.CompilerParams(vmem_limit_bytes=50 * MIB),
        cost_estimate=pl.CostEstimate(
            flops=14 * 10**9, bytes_accessed=18 * MIB, transcendentals=4 * MIB
        ),
    )(pos, lengths, inverse, *pieces, w_tower, w_in, w_out, out_grad)


def rows_kernel(pos, p0, p1, p2, p3, p4, p5, p6, p7, w_tower_h, turned, slope, w_cols, sem):
    me = pos[0]
    load = pltpu.make_async_copy(
        w_tower_h.at[:, pl.ds(pl.multiple_of(me * 128, 128), 128)], w_cols, sem
    )
    load.start()
    load.wait()
    for s, piece in enumerate((p0, p1, p2, p3, p4, p5, p6, p7)):
        at = pl.ds(pl.multiple_of((me ^ s) * 128, 128), 128)
        rows = piece[...]
        pre = dot(rows, w_cols[...])
        slope[at, :] = slope_of(pre, sigmoid(pre))
        turned[:, at] = jnp.transpose(rows)


def rows_of(pos, pieces, w_tower):
    return pl.pallas_call(
        rows_kernel,
        out_shape=[jax.ShapeDtypeStruct((D, SLOTS), BF), jax.ShapeDtypeStruct((SLOTS, 128), F32)],
        in_specs=[SMEM] + [VMEM] * 8 + [ANY],
        out_specs=[VMEM, VMEM],
        scratch_shapes=[pltpu.VMEM((D, 128), BF), pltpu.SemaphoreType.DMA],
        compiler_params=pltpu.CompilerParams(vmem_limit_bytes=16 * MIB),
        cost_estimate=pl.CostEstimate(
            flops=2 * SLOTS * D * 128, bytes_accessed=5 * MIB, transcendentals=SLOTS * 128
        ),
    )(pos, *pieces, w_tower)


def slots_kernel(a0, a1, a2, a3, slope, turned, out):
    total = a0[...].astype(F32) + a1[...].astype(F32) + a2[...].astype(F32) + a3[...].astype(F32)
    pre = (total * slope[...]).astype(BF)
    tower = dot(turned[...], pre).reshape(NODES, LOCALS, 8, 128)
    for l in range(LOCALS):
        mine = pre[l * 128 : (l + 1) * 128].astype(F32).reshape(NODES, 8, 128)
        both = jnp.concatenate([mine, tower[:, l]], axis=1)
        out[:, l] = both.astype(BF)


def slots(a, slope, turned):
    return pl.pallas_call(
        slots_kernel,
        out_shape=jax.ShapeDtypeStruct((NODES, LOCALS, 16, 128), BF),
        in_specs=[VMEM] * 6,
        out_specs=VMEM,
        compiler_params=pltpu.CompilerParams(vmem_limit_bytes=16 * MIB),
        cost_estimate=pl.CostEstimate(
            flops=2 * SLOTS * D * 128, bytes_accessed=5 * MIB, transcendentals=0
        ),
    )(*a, slope, turned)


def total_kernel(arrived, out):
    acc = arrived[0, :, :, :].astype(F32)
    for n in range(1, NODES):
        acc = acc + arrived[n, :, :, :].astype(F32)
    row = jnp.concatenate([acc[j, 8:, :] for j in range(LOCALS)], axis=1).astype(BF)
    for n in range(NODES):
        out[n] = row


def total(arrived):
    return pl.pallas_call(
        total_kernel,
        out_shape=jax.ShapeDtypeStruct((NODES, 8, D), BF),
        in_specs=[VMEM],
        out_specs=VMEM,
        compiler_params=pltpu.CompilerParams(vmem_limit_bytes=8 * MIB),
        cost_estimate=pl.CostEstimate(flops=MIB, bytes_accessed=MIB, transcendentals=0),
    )(arrived)


def content_kernel(wanted, arrived, w_tower, tower_rows, out, handed, pre):
    handed[...] = tower_rows[...]
    for n in range(NODES):
        pre[n * 8 : (n + 1) * 8, :] = jnp.concatenate(
            [arrived[n, j].astype(F32)[:8] for j in range(LOCALS)], axis=1
        )
    rows = dot_nt(pre[...].astype(BF), w_tower[...])
    high = rows.astype(BF)
    low = (rows - high.astype(F32)).astype(BF)
    ids = jnp.transpose(wanted[...].reshape(128, 128))
    sub = lax.broadcasted_iota(jnp.int32, (128, 128), 0)
    for j in range(8):
        hot = jnp.where(ids == sub + j * 128, 1.0, 0.0).astype(BF)
        out[j * 128 : (j + 1) * 128, :] = (dot(hot, high) + dot(hot, low)).astype(BF)


def content_side(wanted, arrived, w_tower, tower_rows):
    return pl.pallas_call(
        content_kernel,
        out_shape=[
            jax.ShapeDtypeStruct((1024, D), BF), jax.ShapeDtypeStruct((NODES, 8, D), BF)
        ],
        in_specs=[VMEM] * 4,
        out_specs=[VMEM, VMEM],
        scratch_shapes=[pltpu.VMEM((128, D), F32)],
        compiler_params=pltpu.CompilerParams(vmem_limit_bytes=16 * MIB),
        cost_estimate=pl.CostEstimate(
            flops=6 * 128 * D * D, bytes_accessed=5 * MIB, transcendentals=0
        ),
    )(wanted, arrived, w_tower, tower_rows)


def tower_kernel(pos, p0, p1, p2, p3, p4, p5, p6, p7, out, buf, sem):
    me = pos[0]
    copies = []
    for s, piece in enumerate((p0, p1, p2, p3, p4, p5, p6, p7)):
        buf[s] = piece[...].astype(F32)
        copies.append(pltpu.make_async_copy(buf.at[s], out.at[:, me ^ s], sem.at[s]))
        copies[-1].start()
    for c in copies:
        c.wait()


def tower_side(pos, pieces):
    return pl.pallas_call(
        tower_kernel,
        out_shape=jax.ShapeDtypeStruct((NODES, LOCALS, 8, D), F32),
        in_specs=[SMEM] + [VMEM] * 8,
        out_specs=ANY,
        scratch_shapes=[pltpu.VMEM((8, NODES, 8, D), F32), pltpu.SemaphoreType.DMA((8,))],
        compiler_params=pltpu.CompilerParams(vmem_limit_bytes=16 * MIB),
        cost_estimate=pl.CostEstimate(flops=MIB, bytes_accessed=6 * MIB, transcendentals=0),
    )(pos, *pieces)


def swap(x, s):
    return lax.ppermute(x, "local", [(i, i ^ s) for i in range(LOCALS)])


def gather_local(x, again=None):
    got = {0: x}
    for s in (4, 2, 6):
        got[s] = swap(x, s)
    if again is not None:
        got[0] = again
    for s in (0, 4, 2, 6):
        got[s + 1] = swap(got[s], 1)
    return [got[s] for s in range(LOCALS)]


def body(inverse, slot_rows, lengths, content, w_tower, w_in, w_out, out_grad):
    pos = lax.axis_index("local").astype(jnp.int32).reshape(1)
    asked = jnp.broadcast_to(slot_rows.reshape(NODES, 8, 1), (NODES, 8, 128))
    wanted = lax.all_to_all(asked, "node", 0, 0, tiled=True)
    picked = pick(wanted, content)
    fetched = lax.all_to_all(picked, "node", 0, 0, tiled=True).reshape(128, D)
    pieces = gather_local(fetched)
    events_out, *blocks = layer(
        pos, lengths, inverse, pieces, w_tower, w_in, w_out, out_grad.reshape(ROWS, D)
    )
    keep, send = blocks[:4], blocks[4:]
    turned, slope = rows_of(pos, pieces, w_tower)
    pair = {k: keep[k] + swap(send[k], 1) for k in (2, 1, 3, 0)}
    arrived = [pair[0]] + [swap(pair[k], 2 * k) for k in (2, 1, 3)]
    out = slots(arrived, slope, turned).reshape(NODES * LOCALS, 16, 128)
    back = lax.all_to_all(out, ("node", "local"), 0, 0, tiled=True).reshape(NODES, LOCALS, 16, 128)
    rows = lax.all_to_all(total(back), "node", 0, 0, tiled=True)
    content_grad, handed = content_side(wanted, back, w_tower, rows)
    tower_grad = tower_side(pos, gather_local(rows, handed)).reshape(D, D)
    return (events_out.reshape(2, SEQ, D), content_grad, tower_grad)


def solution(mesh):
    in_specs = (
        P(("node", "local"), None),
        P("node", "local", None, None),
        P(("node", "local")),
        P(("node", "local"), None),
        P(),
        P(),
        P(),
        P(("node", "local"), None, None),
    )
    out_specs = (P(("node", "local"), None, None), P(("node", "local"), None), P())
    return jax.shard_map(body, mesh=mesh, in_specs=in_specs, out_specs=out_specs, check_vma=False)
```

```python
import functools

import jax
import jax.numpy as jnp
from jax import lax
from jax.experimental import pallas as pl
from jax.experimental.pallas import tpu as pltpu
from jax.sharding import PartitionSpec as P

HEADS = 8
BF = jnp.bfloat16
F32 = jnp.float32
NODES = 16
LOCALS = 8
D = 1024
SLOTS = 1024
ROWS = 512
SEQ = 256
MIB = 1 << 20

VMEM = pl.BlockSpec(memory_space=pltpu.VMEM)
SMEM = pl.BlockSpec(memory_space=pltpu.SMEM)
ANY = pl.BlockSpec(memory_space=pl.ANY)


def dot(a, b):
    return jnp.dot(a, b, preferred_element_type=F32)


def dot_nt(a, b):
    return lax.dot_general(a, b, (((1,), (1,)), ((), ())), preferred_element_type=F32)


def dot_tn(a, b):
    return lax.dot_general(a, b, (((0,), (0,)), ((), ())), preferred_element_type=F32)


def sigmoid(v):
    return 0.5 + 0.5 * jnp.tanh(0.5 * v)


def slope_of(v, sigma):
    return sigma * (1.0 + v * (1.0 - sigma))


def ask_kernel(rows, out):
    for n in range(NODES):
        out[n] = jnp.broadcast_to(rows[:, n : n + 1], (8, 128))


def ask(rows):
    return pl.pallas_call(
        ask_kernel,
        out_shape=jax.ShapeDtypeStruct((NODES, 8, 128), jnp.int32),
        in_specs=[VMEM],
        out_specs=VMEM,
        compiler_params=pltpu.CompilerParams(vmem_limit_bytes=2 * MIB),
        cost_estimate=pl.CostEstimate(flops=20 * 10**9, bytes_accessed=MIB, transcendentals=0),
    )(rows)


def pick_kernel(wanted, content, out):
    ids = wanted[...].reshape(128, 128)
    lane = lax.broadcasted_iota(jnp.int32, (128, 128), 1)
    hot = jnp.concatenate(
        [jnp.where(ids == lane + j * 128, 1.0, 0.0).astype(BF) for j in range(8)], axis=1
    )
    out[...] = dot(hot, content[...]).astype(BF).reshape(NODES, 8, D)


def pick(wanted, content):
    return pl.pallas_call(
        pick_kernel,
        out_shape=jax.ShapeDtypeStruct((NODES, 8, D), BF),
        in_specs=[VMEM, VMEM],
        out_specs=VMEM,
        compiler_params=pltpu.CompilerParams(vmem_limit_bytes=12 * MIB),
        cost_estimate=pl.CostEstimate(flops=2 * 128 * D * D, bytes_accessed=3 * MIB, transcendentals=0),
    )(wanted, content)


def layer_kernel(
    pos, lengths, inverse, p0, p1, p2, p3, p4, p5, p6, p7, w_tower_h, w_in_h, w_out_h, grad_h,
    events_out_h, k0, k1, k2, k3, s0, s1, s2, s3,
    table, w_tower, w_in, w_out, grad, out_buf, events, normed, hidden, slope, attn, attn_slope,
    mixed, half, dgated, dmixed, dpre, coef, inv_rms, hot_gather, hot_scatter, pre_a, pre_b,
    sem_w, sem_in, sem_out,
):
    me = pos[0]
    tower_load = pltpu.make_async_copy(w_tower_h, w_tower, sem_w.at[0])
    out_load = pltpu.make_async_copy(w_out_h, w_out, sem_w.at[1])
    grad_load = pltpu.make_async_copy(grad_h, grad, sem_w.at[2])
    in_loads = [
        pltpu.make_async_copy(
            w_in_h.at[:, pl.ds(j * D, D)], w_in.at[:, pl.ds(j * D, D)], sem_in.at[j]
        )
        for j in range(4)
    ]
    tower_load.start()
    for c in in_loads:
        c.start()
    for s, piece in enumerate((p0, p1, p2, p3, p4, p5, p6, p7)):
        table[pl.ds(pl.multiple_of((me ^ s) * 128, 128), 128), :] = piece[...]

    for b in range(2):
        row = inverse[b : b + 1, :]
        column = jnp.transpose(jnp.broadcast_to(row, (128, SEQ)))
        lane = lax.broadcasted_iota(jnp.int32, (SEQ, 128), 1)
        sub = lax.broadcasted_iota(jnp.int32, (128, SEQ), 0)
        for j in range(8):
            hot_gather[b * SEQ : (b + 1) * SEQ, j * 128 : (j + 1) * 128] = jnp.where(
                column == lane + j * 128, 1.0, 0.0
            ).astype(BF)
            hot_scatter[j * 128 : (j + 1) * 128, b * SEQ : (b + 1) * SEQ] = jnp.where(
                row == sub + j * 128, 1.0, 0.0
            ).astype(BF)
        length = lengths[b]
        query = lax.broadcasted_iota(jnp.int32, (SEQ, SEQ), 0)
        key = lax.broadcasted_iota(jnp.int32, (SEQ, SEQ), 1)
        share = (0.5 * 128 ** (-0.5)) / jnp.full((SEQ, SEQ), length, jnp.int32).astype(F32)
        coef[b] = jnp.where((key <= query) & (query < length), share, 0.0)

    @pl.loop(0, 2)
    def _(c):
        at = pl.ds(pl.multiple_of(c * 512, 512), 512)
        half[:, at] = dot(hot_gather[...], table[:, at]).astype(BF)

    tower_load.wait()

    @pl.loop(0, 2)
    def _(c):
        at = pl.ds(pl.multiple_of(c * 512, 512), 512)
        pre = dot(half[...], w_tower[:, at])
        events[:, at] = (pre * sigmoid(pre)).astype(BF)

    out_load.start()
    grad_load.start()

    @pl.loop(0, 8, unroll=2)
    def _(i):
        at = pl.ds(pl.multiple_of(i * 64, 64), 64)
        x = events[at, :].astype(F32)
        r = lax.rsqrt(jnp.mean(x * x, axis=-1, keepdims=True) + 1e-06)
        inv_rms[at, :] = jnp.broadcast_to(r, (64, 128))
        normed[at, :] = (x * r).astype(BF)

    def product(c, into):
        into[...] = dot(normed[...], w_in[:, pl.ds(pl.multiple_of(c * 256, 256), 256)])

    def activate(c, source):
        at = pl.ds(pl.multiple_of(c * 256, 256), 256)
        pre = source[...]
        sigma = sigmoid(pre)
        act = pre * sigma
        hidden[:, at] = act.astype(BF)
        slope[:, at] = (sigma + act * (1.0 - sigma)).astype(BF)

    in_loads[0].wait()
    in_loads[1].wait()
    product(0, pre_a)
    for j in range(2):

        @pl.loop(4 * j, 4 * j + 3 + j)
        def _(i):
            product(2 * i + 1, pre_b)
            activate(2 * i, pre_a)
            product(jnp.minimum(2 * i + 2, 15), pre_a)
            activate(2 * i + 1, pre_b)

        if j == 0:
            in_loads[2].wait()
            in_loads[3].wait()
            product(7, pre_b)
            activate(6, pre_a)
            product(8, pre_a)
            activate(7, pre_b)

    scale = 128 ** (-0.5)
    out_load.wait()
    grad_load.wait()

    @pl.loop(0, HEADS // 2)
    def _(i):
        jobs = [(2 * i + k, b, slice(b * SEQ, (b + 1) * SEQ)) for k in range(2) for b in range(2)]
        head = lambda h, base: pl.ds(pl.multiple_of(base + h * 128, 128), 128)
        score = lambda h, b, rows: dot_nt(
            hidden[rows, head(h, 2 * D)], hidden[rows, head(h, 3 * D)]
        )
        raw = score(*jobs[0])
        for j, (h, b, rows) in enumerate(jobs):
            later = score(*jobs[j + 1]) if j < 3 else None
            turn = jnp.tanh(raw * (0.5 * scale))
            share = coef[b]
            part = share + share * turn
            weights = raw * part
            attn[h, b] = weights.astype(BF)
            rest = (0.5 * scale) - (0.5 * scale) * turn
            attn_slope[h, b] = (part + weights * rest).astype(BF)
            raw = later
        for h, b, rows in jobs:
            mixed[rows, head(h, 0)] = dot(attn[h, b], hidden[rows, head(h, D)])
        at = pl.ds(pl.multiple_of(i * 256, 256), 256)
        dgated[:, at] = dot_nt(grad[...], w_out[at, :]).astype(BF)

    @pl.loop(0, 8, unroll=2)
    def _(i):
        at = pl.ds(pl.multiple_of(i * 64, 64), 64)
        m = mixed[at, :]
        centred = m - jnp.mean(m, axis=-1, keepdims=True)
        r = lax.rsqrt(jnp.mean(centred * centred, axis=-1, keepdims=True) + 1e-05)
        normal = centred * r
        gate = hidden[at, 0:D].astype(F32)
        half[at, :] = (normal * gate).astype(BF)
        dg = dgated[at, :].astype(F32)
        dgate = (dg * normal).astype(BF).astype(F32)
        dpre[at, 0:D] = (dgate * slope[at, 0:D].astype(F32)).astype(BF)
        dnormal = dg * gate
        m1 = jnp.mean(dnormal, axis=-1, keepdims=True)
        m2 = jnp.mean(dnormal * normal, axis=-1, keepdims=True)
        dmixed[at, :] = (r * (dnormal - m1 - normal * m2)).astype(BF)

    @pl.loop(0, HEADS // 2)
    def _(i):
        jobs = [(2 * i + k, b, slice(b * SEQ, (b + 1) * SEQ)) for k in range(2) for b in range(2)]
        head = lambda h, base: pl.ds(pl.multiple_of(base + h * 128, 128), 128)

        def put(h, rows, base, d):
            d = d.astype(BF).astype(F32) * slope[rows, head(h, base)].astype(F32)
            dpre[rows, head(h, base)] = d.astype(BF)

        dws = [dot_nt(dmixed[rows, head(h, 0)], hidden[rows, head(h, D)]) for h, b, rows in jobs]
        dss = [
            (dw.astype(BF).astype(F32) * attn_slope[h, b].astype(F32)).astype(BF)
            for dw, (h, b, rows) in zip(dws, jobs)
        ]
        for h, b, rows in jobs:
            put(h, rows, D, dot_tn(attn[h, b], dmixed[rows, head(h, 0)]))
        for ds, (h, b, rows) in zip(dss, jobs):
            put(h, rows, 2 * D, dot(ds, hidden[rows, head(h, 3 * D)]))
            put(h, rows, 3 * D, dot_tn(ds, hidden[rows, head(h, 2 * D)]))
        at = pl.ds(pl.multiple_of(i * 256, 256), 256)
        out_buf[:, at] = (events[:, at].astype(F32) + dot(half[...], w_out[:, at])).astype(BF)

    store = pltpu.make_async_copy(out_buf, events_out_h, sem_out)
    store.start()

    @pl.loop(0, 2)
    def _(c):
        at = pl.ds(pl.multiple_of(c * 512, 512), 512)
        mixed[:, at] = dot_nt(dpre[...], w_in[at, :]).astype(BF).astype(F32)

    @pl.loop(0, 8, unroll=2)
    def _(i):
        at = pl.ds(pl.multiple_of(i * 64, 64), 64)
        dn = mixed[at, :]
        r = inv_rms[at, 0:1]
        unit = events[at, :].astype(F32) * r
        dx = r * (dn - unit * jnp.mean(dn * unit, axis=-1, keepdims=True))
        half[at, :] = (grad[at, :].astype(F32) + dx).astype(BF)

    z, core = me // 2, me % 2
    keeps, sends = (k0, k1, k2, k3), (s0, s1, s2, s3)
    for k in range(4):
        at = pl.ds(pl.multiple_of((z ^ k) * 256, 256), 256)
        got = dot(hot_scatter[...], half[:, at])
        even, odd = got[:, :128], got[:, 128:]
        keeps[k][...] = jnp.where(core == 0, even, odd).astype(BF)
        sends[k][...] = jnp.where(core == 0, odd, even).astype(BF)
    store.wait()


def layer(pos, lengths, inverse, pieces, w_tower, w_in, w_out, out_grad):
    block = jax.ShapeDtypeStruct((SLOTS, 128), BF)
    vm = pltpu.VMEM
    return pl.pallas_call(
        layer_kernel,
        out_shape=[jax.ShapeDtypeStruct((ROWS, D), BF)] + [block] * 8,
        in_specs=[SMEM, SMEM] + [VMEM] * 9 + [ANY] * 4,
        out_specs=[ANY] + [VMEM] * 8,
        scratch_shapes=[
            vm((SLOTS, D), BF), vm((D, D), BF), vm((D, 4 * D), BF), vm((D, D), BF), vm((ROWS, D), BF),
            vm((ROWS, D), BF), vm((ROWS, D), BF), vm((ROWS, D), BF), vm((ROWS, 4 * D), BF),
            vm((ROWS, 4 * D), BF), vm((HEADS, 2, SEQ, SEQ), BF), vm((HEADS, 2, SEQ, SEQ), BF),
            vm((ROWS, D), F32), vm((ROWS, D), BF), vm((ROWS, D), BF), vm((ROWS, D), BF), vm((ROWS, 4 * D), BF),
            vm((2, SEQ, SEQ), F32), vm((ROWS, 128), F32),
            vm((ROWS, SLOTS), BF), vm((SLOTS, ROWS), BF),
            vm((ROWS, 256), F32), vm((ROWS, 256), F32),
            pltpu.SemaphoreType.DMA((3,)), pltpu.SemaphoreType.DMA((4,)), pltpu.SemaphoreType.DMA,
        ],
        compiler_params=pltpu.CompilerParams(vmem_limit_bytes=50 * MIB),
        cost_estimate=pl.CostEstimate(
            flops=14 * 10**9, bytes_accessed=18 * MIB, transcendentals=4 * MIB
        ),
    )(pos, lengths, inverse, *pieces, w_tower, w_in, w_out, out_grad)


def rows_kernel(pos, p0, p1, p2, p3, p4, p5, p6, p7, w_tower_h, turned, slope, w_cols, sem):
    me = pos[0]
    load = pltpu.make_async_copy(
        w_tower_h.at[:, pl.ds(pl.multiple_of(me * 128, 128), 128)], w_cols, sem
    )
    load.start()
    load.wait()
    for s, piece in enumerate((p0, p1, p2, p3, p4, p5, p6, p7)):
        at = pl.ds(pl.multiple_of((me ^ s) * 128, 128), 128)
        rows = piece[...]
        pre = dot(rows, w_cols[...])
        slope[at, :] = slope_of(pre, sigmoid(pre))
        turned[:, at] = jnp.transpose(rows)


def rows_of(pos, pieces, w_tower):
    return pl.pallas_call(
        rows_kernel,
        out_shape=[jax.ShapeDtypeStruct((D, SLOTS), BF), jax.ShapeDtypeStruct((SLOTS, 128), F32)],
        in_specs=[SMEM] + [VMEM] * 8 + [ANY],
        out_specs=[VMEM, VMEM],
        scratch_shapes=[pltpu.VMEM((D, 128), BF), pltpu.SemaphoreType.DMA],
        compiler_params=pltpu.CompilerParams(vmem_limit_bytes=16 * MIB),
        cost_estimate=pl.CostEstimate(
            flops=2 * SLOTS * D * 128, bytes_accessed=5 * MIB, transcendentals=SLOTS * 128
        ),
    )(pos, *pieces, w_tower)


def slots_kernel(a0, a1, a2, a3, slope, turned, out):
    total = a0[...].astype(F32) + a1[...].astype(F32) + a2[...].astype(F32) + a3[...].astype(F32)
    pre = (total * slope[...]).astype(BF)
    tower = dot(turned[...], pre).reshape(NODES, LOCALS, 8, 128)
    for l in range(LOCALS):
        mine = pre[l * 128 : (l + 1) * 128].astype(F32).reshape(NODES, 8, 128)
        both = jnp.concatenate([mine, tower[:, l]], axis=1)
        out[:, l] = both.astype(BF)


def slots(a, slope, turned):
    return pl.pallas_call(
        slots_kernel,
        out_shape=jax.ShapeDtypeStruct((NODES, LOCALS, 16, 128), BF),
        in_specs=[VMEM] * 6,
        out_specs=VMEM,
        compiler_params=pltpu.CompilerParams(vmem_limit_bytes=16 * MIB),
        cost_estimate=pl.CostEstimate(
            flops=2 * SLOTS * D * 128, bytes_accessed=5 * MIB, transcendentals=0
        ),
    )(*a, slope, turned)


def total_kernel(arrived, out):
    acc = arrived[0, :, :, :].astype(F32)
    for n in range(1, NODES):
        acc = acc + arrived[n, :, :, :].astype(F32)
    row = jnp.concatenate([acc[j, 8:, :] for j in range(LOCALS)], axis=1).astype(BF)
    for n in range(NODES):
        out[n] = row


def total(arrived):
    return pl.pallas_call(
        total_kernel,
        out_shape=jax.ShapeDtypeStruct((NODES, 8, D), BF),
        in_specs=[VMEM],
        out_specs=VMEM,
        compiler_params=pltpu.CompilerParams(vmem_limit_bytes=8 * MIB),
        cost_estimate=pl.CostEstimate(flops=MIB, bytes_accessed=MIB, transcendentals=0),
    )(arrived)


def content_kernel(wanted, arrived, w_tower, tower_rows, out, handed, pre):
    handed[...] = tower_rows[...]
    for n in range(NODES):
        pre[n * 8 : (n + 1) * 8, :] = jnp.concatenate(
            [arrived[n, j].astype(F32)[:8] for j in range(LOCALS)], axis=1
        )
    rows = dot_nt(pre[...].astype(BF), w_tower[...])
    high = rows.astype(BF)
    low = (rows - high.astype(F32)).astype(BF)
    ids = jnp.transpose(wanted[...].reshape(128, 128))
    sub = lax.broadcasted_iota(jnp.int32, (128, 128), 0)
    for j in range(8):
        hot = jnp.where(ids == sub + j * 128, 1.0, 0.0).astype(BF)
        out[j * 128 : (j + 1) * 128, :] = (dot(hot, high) + dot(hot, low)).astype(BF)


def content_side(wanted, arrived, w_tower, tower_rows):
    return pl.pallas_call(
        content_kernel,
        out_shape=[
            jax.ShapeDtypeStruct((1024, D), BF), jax.ShapeDtypeStruct((NODES, 8, D), BF)
        ],
        in_specs=[VMEM] * 4,
        out_specs=[VMEM, VMEM],
        scratch_shapes=[pltpu.VMEM((128, D), F32)],
        compiler_params=pltpu.CompilerParams(vmem_limit_bytes=16 * MIB),
        cost_estimate=pl.CostEstimate(
            flops=6 * 128 * D * D, bytes_accessed=5 * MIB, transcendentals=0
        ),
    )(wanted, arrived, w_tower, tower_rows)


def tower_kernel(pos, p0, p1, p2, p3, p4, p5, p6, p7, out, buf, sem):
    me = pos[0]
    copies = []
    for s, piece in enumerate((p0, p1, p2, p3, p4, p5, p6, p7)):
        buf[s] = piece[...].astype(F32)
        copies.append(pltpu.make_async_copy(buf.at[s], out.at[:, me ^ s], sem.at[s]))
        copies[-1].start()
    for c in copies:
        c.wait()


def tower_side(pos, pieces):
    return pl.pallas_call(
        tower_kernel,
        out_shape=jax.ShapeDtypeStruct((NODES, LOCALS, 8, D), F32),
        in_specs=[SMEM] + [VMEM] * 8,
        out_specs=ANY,
        scratch_shapes=[pltpu.VMEM((8, NODES, 8, D), F32), pltpu.SemaphoreType.DMA((8,))],
        compiler_params=pltpu.CompilerParams(vmem_limit_bytes=16 * MIB),
        cost_estimate=pl.CostEstimate(flops=MIB, bytes_accessed=6 * MIB, transcendentals=0),
    )(pos, *pieces)


def swap(x, s):
    return lax.ppermute(x, "local", [(i, i ^ s) for i in range(LOCALS)])


def gather_local(x, again=None):
    got = {0: x}
    for s in (4, 2, 6):
        got[s] = swap(x, s)
    if again is not None:
        got[0] = again
    for s in (0, 4, 2, 6):
        got[s + 1] = swap(got[s], 1)
    return [got[s] for s in range(LOCALS)]


def body(inverse, slot_rows, lengths, content, w_tower, w_in, w_out, out_grad):
    pos = lax.axis_index("local").astype(jnp.int32).reshape(1)
    asked = ask(slot_rows.reshape(NODES, 8).T)
    wanted = lax.all_to_all(asked, "node", 0, 0, tiled=True)
    picked = pick(wanted, content)
    fetched = lax.all_to_all(picked, "node", 0, 0, tiled=True).reshape(128, D)
    pieces = gather_local(fetched)
    events_out, *blocks = layer(
        pos, lengths, inverse, pieces, w_tower, w_in, w_out, out_grad.reshape(ROWS, D)
    )
    keep, send = blocks[:4], blocks[4:]
    turned, slope = rows_of(pos, pieces, w_tower)
    pair = {k: keep[k] + swap(send[k], 1) for k in (2, 1, 3, 0)}
    arrived = [pair[0]] + [swap(pair[k], 2 * k) for k in (2, 1, 3)]
    out = slots(arrived, slope, turned).reshape(NODES * LOCALS, 16, 128)
    back = lax.all_to_all(out, ("node", "local"), 0, 0, tiled=True).reshape(NODES, LOCALS, 16, 128)
    rows = lax.all_to_all(total(back), "node", 0, 0, tiled=True)
    content_grad, handed = content_side(wanted, back, w_tower, rows)
    tower_grad = tower_side(pos, gather_local(rows, handed)).reshape(D, D)
    return (events_out.reshape(2, SEQ, D), content_grad, tower_grad)


def solution(mesh):
    in_specs = (
        P(("node", "local"), None),
        P("node", "local", None, None),
        P(("node", "local")),
        P(("node", "local"), None),
        P(),
        P(),
        P(),
        P(("node", "local"), None, None),
    )
    out_specs = (P(("node", "local"), None, None), P(("node", "local"), None), P())
    return jax.shard_map(body, mesh=mesh, in_specs=in_specs, out_specs=out_specs, check_vma=False)
```

```python
import functools

import jax
import jax.numpy as jnp
from jax import lax
from jax.experimental import pallas as pl
from jax.experimental.pallas import tpu as pltpu
from jax.sharding import PartitionSpec as P

HEADS = 8
BF = jnp.bfloat16
F32 = jnp.float32
NODES = 16
LOCALS = 8
D = 1024
SLOTS = 1024
ROWS = 512
SEQ = 256
MIB = 1 << 20

VMEM = pl.BlockSpec(memory_space=pltpu.VMEM)
SMEM = pl.BlockSpec(memory_space=pltpu.SMEM)
ANY = pl.BlockSpec(memory_space=pl.ANY)


def dot(a, b):
    return jnp.dot(a, b, preferred_element_type=F32)


def dot_nt(a, b):
    return lax.dot_general(a, b, (((1,), (1,)), ((), ())), preferred_element_type=F32)


def dot_tn(a, b):
    return lax.dot_general(a, b, (((0,), (0,)), ((), ())), preferred_element_type=F32)


def sigmoid(v):
    return 0.5 + 0.5 * jnp.tanh(0.5 * v)


def slope_of(v, sigma):
    return sigma * (1.0 + v * (1.0 - sigma))


def ask_kernel(rows, out):
    for n in range(NODES):
        out[n] = jnp.broadcast_to(rows[:, n : n + 1], (8, 128))


def ask(rows):
    return pl.pallas_call(
        ask_kernel,
        out_shape=jax.ShapeDtypeStruct((NODES, 8, 128), jnp.int32),
        in_specs=[VMEM],
        out_specs=VMEM,
        compiler_params=pltpu.CompilerParams(vmem_limit_bytes=2 * MIB),
        cost_estimate=pl.CostEstimate(flops=20 * 10**9, bytes_accessed=MIB, transcendentals=0),
    )(rows)


def pick_kernel(wanted, content, out):
    ids = wanted[...].reshape(128, 128)
    lane = lax.broadcasted_iota(jnp.int32, (128, 128), 1)
    hot = jnp.concatenate(
        [jnp.where(ids == lane + j * 128, 1.0, 0.0).astype(BF) for j in range(8)], axis=1
    )
    out[...] = dot(hot, content[...]).astype(BF).reshape(NODES, 8, D)


def pick(wanted, content):
    return pl.pallas_call(
        pick_kernel,
        out_shape=jax.ShapeDtypeStruct((NODES, 8, D), BF),
        in_specs=[VMEM, VMEM],
        out_specs=VMEM,
        compiler_params=pltpu.CompilerParams(vmem_limit_bytes=12 * MIB),
        cost_estimate=pl.CostEstimate(flops=2 * 128 * D * D, bytes_accessed=3 * MIB, transcendentals=0),
    )(wanted, content)


def layer_kernel(
    pos, lengths, inverse, p0, p1, p2, p3, p4, p5, p6, p7, w_tower_h, w_in_h, w_out_h, grad_h,
    events_out_h, k0, k1, k2, k3, s0, s1, s2, s3,
    table, w_tower, w_in, w_out, grad, out_buf, events, normed, hidden, slope, attn, attn_slope,
    mixed, half, dgated, dmixed, dpre, coef, inv_rms, hot_gather, hot_scatter, pre_a, pre_b,
    sem_w, sem_in, sem_out,
):
    me = pos[0]
    tower_load = pltpu.make_async_copy(w_tower_h, w_tower, sem_w.at[0])
    out_load = pltpu.make_async_copy(w_out_h, w_out, sem_w.at[1])
    grad_load = pltpu.make_async_copy(grad_h, grad, sem_w.at[2])
    in_loads = [
        pltpu.make_async_copy(
            w_in_h.at[:, pl.ds(j * D, D)], w_in.at[:, pl.ds(j * D, D)], sem_in.at[j]
        )
        for j in range(4)
    ]
    tower_load.start()
    for c in in_loads:
        c.start()
    for s, piece in enumerate((p0, p1, p2, p3, p4, p5, p6, p7)):
        table[pl.ds(pl.multiple_of((me ^ s) * 128, 128), 128), :] = piece[...]

    for b in range(2):
        row = inverse[b : b + 1, :]
        column = jnp.transpose(jnp.broadcast_to(row, (128, SEQ)))
        lane = lax.broadcasted_iota(jnp.int32, (SEQ, 128), 1)
        sub = lax.broadcasted_iota(jnp.int32, (128, SEQ), 0)
        for j in range(8):
            hot_gather[b * SEQ : (b + 1) * SEQ, j * 128 : (j + 1) * 128] = jnp.where(
                column == lane + j * 128, 1.0, 0.0
            ).astype(BF)
            hot_scatter[j * 128 : (j + 1) * 128, b * SEQ : (b + 1) * SEQ] = jnp.where(
                row == sub + j * 128, 1.0, 0.0
            ).astype(BF)
        length = lengths[b]
        query = lax.broadcasted_iota(jnp.int32, (SEQ, SEQ), 0)
        key = lax.broadcasted_iota(jnp.int32, (SEQ, SEQ), 1)
        share = (0.5 * 128 ** (-0.5)) / jnp.full((SEQ, SEQ), length, jnp.int32).astype(F32)
        coef[b] = jnp.where((key <= query) & (query < length), share, 0.0)

    @pl.loop(0, 2)
    def _(c):
        at = pl.ds(pl.multiple_of(c * 512, 512), 512)
        half[:, at] = dot(hot_gather[...], table[:, at]).astype(BF)

    tower_load.wait()

    @pl.loop(0, 2)
    def _(c):
        at = pl.ds(pl.multiple_of(c * 512, 512), 512)
        pre = dot(half[...], w_tower[:, at])
        events[:, at] = (pre * sigmoid(pre)).astype(BF)

    out_load.start()
    grad_load.start()

    @pl.loop(0, 4, unroll=1)
    def _(i):
        at = pl.ds(pl.multiple_of(i * 128, 128), 128)
        x = events[at, :].astype(F32)
        r = lax.rsqrt(jnp.mean(x * x, axis=-1, keepdims=True) + 1e-06)
        inv_rms[at, :] = jnp.broadcast_to(r, (128, 128))
        normed[at, :] = (x * r).astype(BF)

    def product(c, into):
        into[...] = dot(normed[...], w_in[:, pl.ds(pl.multiple_of(c * 512, 512), 512)])

    def activate(c, source):
        at = pl.ds(pl.multiple_of(c * 512, 512), 512)
        pre = source[...]
        sigma = sigmoid(pre)
        act = pre * sigma
        hidden[:, at] = act.astype(BF)
        slope[:, at] = (sigma + act * (1.0 - sigma)).astype(BF)

    for c in in_loads:
        c.wait()
    product(0, pre_a)

    @pl.loop(0, 3)
    def _(i):
        product(2 * i + 1, pre_b)
        activate(2 * i, pre_a)
        product(2 * i + 2, pre_a)
        activate(2 * i + 1, pre_b)

    product(7, pre_b)
    activate(6, pre_a)
    activate(7, pre_b)

    scale = 128 ** (-0.5)
    out_load.wait()
    grad_load.wait()

    @pl.loop(0, HEADS // 2)
    def _(i):
        jobs = [(2 * i + k, b, slice(b * SEQ, (b + 1) * SEQ)) for k in range(2) for b in range(2)]
        head = lambda h, base: pl.ds(pl.multiple_of(base + h * 128, 128), 128)
        score = lambda h, b, rows: dot_nt(
            hidden[rows, head(h, 2 * D)], hidden[rows, head(h, 3 * D)]
        )
        raw = score(*jobs[0])
        for j, (h, b, rows) in enumerate(jobs):
            later = score(*jobs[j + 1]) if j < 3 else None
            turn = jnp.tanh(raw * (0.5 * scale))
            share = coef[b]
            part = share + share * turn
            weights = raw * part
            attn[h, b] = weights.astype(BF)
            rest = (0.5 * scale) - (0.5 * scale) * turn
            attn_slope[h, b] = (part + weights * rest).astype(BF)
            raw = later
        for h, b, rows in jobs:
            mixed[rows, head(h, 0)] = dot(attn[h, b], hidden[rows, head(h, D)])
        at = pl.ds(pl.multiple_of(i * 256, 256), 256)
        dgated[:, at] = dot_nt(grad[...], w_out[at, :]).astype(BF)

    @pl.loop(0, 8, unroll=2)
    def _(i):
        at = pl.ds(pl.multiple_of(i * 64, 64), 64)
        m = mixed[at, :]
        centred = m - jnp.mean(m, axis=-1, keepdims=True)
        r = lax.rsqrt(jnp.mean(centred * centred, axis=-1, keepdims=True) + 1e-05)
        normal = centred * r
        gate = hidden[at, 0:D].astype(F32)
        half[at, :] = (normal * gate).astype(BF)
        dg = dgated[at, :].astype(F32)
        dpre[at, 0:D] = (dg * normal).astype(BF) * slope[at, 0:D]
        dnormal = dg * gate
        m1 = jnp.mean(dnormal, axis=-1, keepdims=True)
        m2 = jnp.mean(dnormal * normal, axis=-1, keepdims=True)
        dmixed[at, :] = (r * (dnormal - m1 - normal * m2)).astype(BF)

    @pl.loop(0, HEADS // 2)
    def _(i):
        jobs = [(2 * i + k, b, slice(b * SEQ, (b + 1) * SEQ)) for k in range(2) for b in range(2)]
        head = lambda h, base: pl.ds(pl.multiple_of(base + h * 128, 128), 128)

        def put(h, rows, base, d):
            dpre[rows, head(h, base)] = d.astype(BF) * slope[rows, head(h, base)]

        dws = [dot_nt(dmixed[rows, head(h, 0)], hidden[rows, head(h, D)]) for h, b, rows in jobs]
        dss = [
            dw.astype(BF) * attn_slope[h, b]
            for dw, (h, b, rows) in zip(dws, jobs)
        ]
        for h, b, rows in jobs:
            put(h, rows, D, dot_tn(attn[h, b], dmixed[rows, head(h, 0)]))
        for ds, (h, b, rows) in zip(dss, jobs):
            put(h, rows, 2 * D, dot(ds, hidden[rows, head(h, 3 * D)]))
            put(h, rows, 3 * D, dot_tn(ds, hidden[rows, head(h, 2 * D)]))
        at = pl.ds(pl.multiple_of(i * 256, 256), 256)
        out_buf[:, at] = (events[:, at].astype(F32) + dot(half[...], w_out[:, at])).astype(BF)

    store = pltpu.make_async_copy(out_buf, events_out_h, sem_out)
    store.start()

    @pl.loop(0, 2)
    def _(c):
        at = pl.ds(pl.multiple_of(c * 512, 512), 512)
        normed[:, at] = dot_nt(dpre[...], w_in[at, :]).astype(BF)

    @pl.loop(0, 4, unroll=1)
    def _(i):
        at = pl.ds(pl.multiple_of(i * 128, 128), 128)
        dn = normed[at, :].astype(F32)
        r = inv_rms[at, 0:1]
        unit = events[at, :].astype(F32) * r
        dx = r * (dn - unit * jnp.mean(dn * unit, axis=-1, keepdims=True))
        half[at, :] = (grad[at, :].astype(F32) + dx).astype(BF)

    z, core = me // 2, me % 2
    keeps, sends = (k0, k1, k2, k3), (s0, s1, s2, s3)
    for k in range(4):
        at = pl.ds(pl.multiple_of((z ^ k) * 256, 256), 256)
        got = dot(hot_scatter[...], half[:, at])
        even, odd = got[:, :128], got[:, 128:]
        keeps[k][...] = jnp.where(core == 0, even, odd).astype(BF)
        sends[k][...] = jnp.where(core == 0, odd, even).astype(BF)
    store.wait()


def layer(pos, lengths, inverse, pieces, w_tower, w_in, w_out, out_grad):
    block = jax.ShapeDtypeStruct((SLOTS, 128), BF)
    vm = pltpu.VMEM
    return pl.pallas_call(
        layer_kernel,
        out_shape=[jax.ShapeDtypeStruct((ROWS, D), BF)] + [block] * 8,
        in_specs=[SMEM, SMEM] + [VMEM] * 9 + [ANY] * 4,
        out_specs=[ANY] + [VMEM] * 8,
        scratch_shapes=[
            vm((SLOTS, D), BF), vm((D, D), BF), vm((D, 4 * D), BF), vm((D, D), BF), vm((ROWS, D), BF),
            vm((ROWS, D), BF), vm((ROWS, D), BF), vm((ROWS, D), BF), vm((ROWS, 4 * D), BF),
            vm((ROWS, 4 * D), BF), vm((HEADS, 2, SEQ, SEQ), BF), vm((HEADS, 2, SEQ, SEQ), BF),
            vm((ROWS, D), F32), vm((ROWS, D), BF), vm((ROWS, D), BF), vm((ROWS, D), BF), vm((ROWS, 4 * D), BF),
            vm((2, SEQ, SEQ), F32), vm((ROWS, 128), F32),
            vm((ROWS, SLOTS), BF), vm((SLOTS, ROWS), BF),
            vm((ROWS, 512), F32), vm((ROWS, 512), F32),
            pltpu.SemaphoreType.DMA((3,)), pltpu.SemaphoreType.DMA((4,)), pltpu.SemaphoreType.DMA,
        ],
        compiler_params=pltpu.CompilerParams(vmem_limit_bytes=50 * MIB),
        cost_estimate=pl.CostEstimate(
            flops=14 * 10**9, bytes_accessed=18 * MIB, transcendentals=4 * MIB
        ),
    )(pos, lengths, inverse, *pieces, w_tower, w_in, w_out, out_grad)


def rows_kernel(pos, p0, p1, p2, p3, p4, p5, p6, p7, w_tower_h, turned, slope, w_cols, sem):
    me = pos[0]
    load = pltpu.make_async_copy(
        w_tower_h.at[:, pl.ds(pl.multiple_of(me * 128, 128), 128)], w_cols, sem
    )
    load.start()
    load.wait()
    for s, piece in enumerate((p0, p1, p2, p3, p4, p5, p6, p7)):
        at = pl.ds(pl.multiple_of((me ^ s) * 128, 128), 128)
        rows = piece[...]
        pre = dot(rows, w_cols[...])
        slope[at, :] = slope_of(pre, sigmoid(pre))
        turned[:, at] = jnp.transpose(rows)


def rows_of(pos, pieces, w_tower):
    return pl.pallas_call(
        rows_kernel,
        out_shape=[jax.ShapeDtypeStruct((D, SLOTS), BF), jax.ShapeDtypeStruct((SLOTS, 128), F32)],
        in_specs=[SMEM] + [VMEM] * 8 + [ANY],
        out_specs=[VMEM, VMEM],
        scratch_shapes=[pltpu.VMEM((D, 128), BF), pltpu.SemaphoreType.DMA],
        compiler_params=pltpu.CompilerParams(vmem_limit_bytes=16 * MIB),
        cost_estimate=pl.CostEstimate(
            flops=2 * SLOTS * D * 128, bytes_accessed=5 * MIB, transcendentals=SLOTS * 128
        ),
    )(pos, *pieces, w_tower)


def slots_kernel(a0, a1, a2, a3, slope, turned, out):
    total = a0[...].astype(F32) + a1[...].astype(F32) + a2[...].astype(F32) + a3[...].astype(F32)
    pre = (total * slope[...]).astype(BF)
    tower = dot(turned[...], pre).reshape(NODES, LOCALS, 8, 128)
    for l in range(LOCALS):
        mine = pre[l * 128 : (l + 1) * 128].astype(F32).reshape(NODES, 8, 128)
        both = jnp.concatenate([mine, tower[:, l]], axis=1)
        out[:, l] = both.astype(BF)


def slots(a, slope, turned):
    return pl.pallas_call(
        slots_kernel,
        out_shape=jax.ShapeDtypeStruct((NODES, LOCALS, 16, 128), BF),
        in_specs=[VMEM] * 6,
        out_specs=VMEM,
        compiler_params=pltpu.CompilerParams(vmem_limit_bytes=16 * MIB),
        cost_estimate=pl.CostEstimate(
            flops=2 * SLOTS * D * 128, bytes_accessed=5 * MIB, transcendentals=0
        ),
    )(*a, slope, turned)


def total_kernel(arrived, out):
    acc = arrived[0, :, :, :].astype(F32)
    for n in range(1, NODES):
        acc = acc + arrived[n, :, :, :].astype(F32)
    row = jnp.concatenate([acc[j, 8:, :] for j in range(LOCALS)], axis=1).astype(BF)
    for n in range(NODES):
        out[n] = row


def total(arrived):
    return pl.pallas_call(
        total_kernel,
        out_shape=jax.ShapeDtypeStruct((NODES, 8, D), BF),
        in_specs=[VMEM],
        out_specs=VMEM,
        compiler_params=pltpu.CompilerParams(vmem_limit_bytes=8 * MIB),
        cost_estimate=pl.CostEstimate(flops=MIB, bytes_accessed=MIB, transcendentals=0),
    )(arrived)


def content_kernel(wanted, arrived, w_tower, tower_rows, out, handed, pre):
    handed[...] = tower_rows[...]
    for n in range(NODES):
        pre[n * 8 : (n + 1) * 8, :] = jnp.concatenate(
            [arrived[n, j].astype(F32)[:8] for j in range(LOCALS)], axis=1
        )
    rows = dot_nt(pre[...].astype(BF), w_tower[...])
    high = rows.astype(BF)
    low = (rows - high.astype(F32)).astype(BF)
    ids = jnp.transpose(wanted[...].reshape(128, 128))
    sub = lax.broadcasted_iota(jnp.int32, (128, 128), 0)
    for j in range(8):
        hot = jnp.where(ids == sub + j * 128, 1.0, 0.0).astype(BF)
        out[j * 128 : (j + 1) * 128, :] = (dot(hot, high) + dot(hot, low)).astype(BF)


def content_side(wanted, arrived, w_tower, tower_rows):
    return pl.pallas_call(
        content_kernel,
        out_shape=[
            jax.ShapeDtypeStruct((1024, D), BF), jax.ShapeDtypeStruct((NODES, 8, D), BF)
        ],
        in_specs=[VMEM] * 4,
        out_specs=[VMEM, VMEM],
        scratch_shapes=[pltpu.VMEM((128, D), F32)],
        compiler_params=pltpu.CompilerParams(vmem_limit_bytes=16 * MIB),
        cost_estimate=pl.CostEstimate(
            flops=6 * 128 * D * D, bytes_accessed=5 * MIB, transcendentals=0
        ),
    )(wanted, arrived, w_tower, tower_rows)


def tower_kernel(pos, p0, p1, p2, p3, p4, p5, p6, p7, out, buf, sem):
    me = pos[0]
    copies = []
    for s, piece in enumerate((p0, p1, p2, p3, p4, p5, p6, p7)):
        buf[s] = piece[...].astype(F32)
        copies.append(pltpu.make_async_copy(buf.at[s], out.at[:, me ^ s], sem.at[s]))
        copies[-1].start()
    for c in copies:
        c.wait()


def tower_side(pos, pieces):
    return pl.pallas_call(
        tower_kernel,
        out_shape=jax.ShapeDtypeStruct((NODES, LOCALS, 8, D), F32),
        in_specs=[SMEM] + [VMEM] * 8,
        out_specs=ANY,
        scratch_shapes=[pltpu.VMEM((8, NODES, 8, D), F32), pltpu.SemaphoreType.DMA((8,))],
        compiler_params=pltpu.CompilerParams(vmem_limit_bytes=16 * MIB),
        cost_estimate=pl.CostEstimate(flops=MIB, bytes_accessed=6 * MIB, transcendentals=0),
    )(pos, *pieces)


def swap(x, s):
    return lax.ppermute(x, "local", [(i, i ^ s) for i in range(LOCALS)])


def gather_local(x, again=None):
    got = {0: x}
    for s in (4, 2, 6):
        got[s] = swap(x, s)
    if again is not None:
        got[0] = again
    for s in (0, 4, 2, 6):
        got[s + 1] = swap(got[s], 1)
    return [got[s] for s in range(LOCALS)]


def body(inverse, slot_rows, lengths, content, w_tower, w_in, w_out, out_grad):
    pos = lax.axis_index("local").astype(jnp.int32).reshape(1)
    asked = ask(slot_rows.reshape(NODES, 8).T)
    wanted = lax.all_to_all(asked, "node", 0, 0, tiled=True)
    picked = pick(wanted, content)
    fetched = lax.all_to_all(picked, "node", 0, 0, tiled=True).reshape(128, D)
    pieces = gather_local(fetched)
    events_out, *blocks = layer(
        pos, lengths, inverse, pieces, w_tower, w_in, w_out, out_grad.reshape(ROWS, D)
    )
    keep, send = blocks[:4], blocks[4:]
    turned, slope = rows_of(pos, pieces, w_tower)
    pair = {k: keep[k] + swap(send[k], 1) for k in (2, 1, 3, 0)}
    arrived = [pair[0]] + [swap(pair[k], 2 * k) for k in (2, 1, 3)]
    out = slots(arrived, slope, turned).reshape(NODES * LOCALS, 16, 128)
    back = lax.all_to_all(out, ("node", "local"), 0, 0, tiled=True).reshape(NODES, LOCALS, 16, 128)
    rows = lax.all_to_all(total(back), "node", 0, 0, tiled=True)
    content_grad, handed = content_side(wanted, back, w_tower, rows)
    tower_grad = tower_side(pos, gather_local(rows, handed)).reshape(D, D)
    return (events_out.reshape(2, SEQ, D), content_grad, tower_grad)


def solution(mesh):
    in_specs = (
        P(("node", "local"), None),
        P("node", "local", None, None),
        P(("node", "local")),
        P(("node", "local"), None),
        P(),
        P(),
        P(),
        P(("node", "local"), None, None),
    )
    out_specs = (P(("node", "local"), None, None), P(("node", "local"), None), P())
    return jax.shard_map(body, mesh=mesh, in_specs=in_specs, out_specs=out_specs, check_vma=False)
```

```python
import functools

import jax
import jax.numpy as jnp
from jax import lax
from jax.experimental import pallas as pl
from jax.experimental.pallas import tpu as pltpu
from jax.sharding import PartitionSpec as P

HEADS = 8
BF = jnp.bfloat16
F32 = jnp.float32
NODES = 16
LOCALS = 8
D = 1024
SLOTS = 1024
ROWS = 512
SEQ = 256
MIB = 1 << 20

VMEM = pl.BlockSpec(memory_space=pltpu.VMEM)
SMEM = pl.BlockSpec(memory_space=pltpu.SMEM)
ANY = pl.BlockSpec(memory_space=pl.ANY)


def dot(a, b):
    return jnp.dot(a, b, preferred_element_type=F32)


def dot_nt(a, b):
    return lax.dot_general(a, b, (((1,), (1,)), ((), ())), preferred_element_type=F32)


def dot_tn(a, b):
    return lax.dot_general(a, b, (((0,), (0,)), ((), ())), preferred_element_type=F32)


def sigmoid(v):
    return 0.5 + 0.5 * jnp.tanh(0.5 * v)


def slope_of(v, sigma):
    return sigma * (1.0 + v * (1.0 - sigma))


def ask_kernel(rows, out):
    for n in range(NODES):
        out[n] = jnp.broadcast_to(rows[:, n : n + 1], (8, 128))


def ask(rows):
    return pl.pallas_call(
        ask_kernel,
        out_shape=jax.ShapeDtypeStruct((NODES, 8, 128), jnp.int32),
        in_specs=[VMEM],
        out_specs=VMEM,
        compiler_params=pltpu.CompilerParams(vmem_limit_bytes=2 * MIB),
        cost_estimate=pl.CostEstimate(flops=20 * 10**9, bytes_accessed=MIB, transcendentals=0),
    )(rows)


def pick_kernel(wanted, content, out):
    ids = wanted[...].reshape(128, 128)
    lane = lax.broadcasted_iota(jnp.int32, (128, 128), 1)
    hot = jnp.concatenate(
        [jnp.where(ids == lane + j * 128, 1.0, 0.0).astype(BF) for j in range(8)], axis=1
    )
    out[...] = dot(hot, content[...]).astype(BF).reshape(NODES, 8, D)


def pick(wanted, content):
    return pl.pallas_call(
        pick_kernel,
        out_shape=jax.ShapeDtypeStruct((NODES, 8, D), BF),
        in_specs=[VMEM, VMEM],
        out_specs=VMEM,
        compiler_params=pltpu.CompilerParams(vmem_limit_bytes=12 * MIB),
        cost_estimate=pl.CostEstimate(flops=2 * 128 * D * D, bytes_accessed=3 * MIB, transcendentals=0),
    )(wanted, content)


def layer_kernel(
    pos, lengths, inverse, p0, p1, p2, p3, p4, p5, p6, p7, w_tower_h, w_in_h, w_out_h, grad_h,
    events_out_h, k0, k1, k2, k3, s0, s1, s2, s3,
    table, w_tower, w_in, w_out, grad, out_buf, events, normed, hidden, slope, attn, attn_slope,
    mixed, half, dgated, dmixed, dpre, coef, inv_rms, hot_gather, hot_scatter, pre_a, pre_b,
    sem_w, sem_in, sem_out,
):
    me = pos[0]
    tower_load = pltpu.make_async_copy(w_tower_h, w_tower, sem_w.at[0])
    out_load = pltpu.make_async_copy(w_out_h, w_out, sem_w.at[1])
    grad_load = pltpu.make_async_copy(grad_h, grad, sem_w.at[2])
    in_loads = [
        pltpu.make_async_copy(
            w_in_h.at[:, pl.ds(j * D, D)], w_in.at[:, pl.ds(j * D, D)], sem_in.at[j]
        )
        for j in range(4)
    ]
    tower_load.start()
    for c in in_loads:
        c.start()
    for s, piece in enumerate((p0, p1, p2, p3, p4, p5, p6, p7)):
        table[pl.ds(pl.multiple_of((me ^ s) * 128, 128), 128), :] = piece[...]

    for b in range(2):
        row = inverse[b : b + 1, :]
        column = jnp.transpose(jnp.broadcast_to(row, (128, SEQ)))
        lane = lax.broadcasted_iota(jnp.int32, (SEQ, 128), 1)
        sub = lax.broadcasted_iota(jnp.int32, (128, SEQ), 0)
        for j in range(8):
            hot_gather[b * SEQ : (b + 1) * SEQ, j * 128 : (j + 1) * 128] = jnp.where(
                column == lane + j * 128, 1.0, 0.0
            ).astype(BF)
            hot_scatter[j * 128 : (j + 1) * 128, b * SEQ : (b + 1) * SEQ] = jnp.where(
                row == sub + j * 128, 1.0, 0.0
            ).astype(BF)
        length = lengths[b]
        query = lax.broadcasted_iota(jnp.int32, (SEQ, SEQ), 0)
        key = lax.broadcasted_iota(jnp.int32, (SEQ, SEQ), 1)
        share = (0.5 * 128 ** (-0.5)) / jnp.full((SEQ, SEQ), length, jnp.int32).astype(F32)
        coef[b] = jnp.where((key <= query) & (query < length), share, 0.0)

    @pl.loop(0, 2)
    def _(c):
        at = pl.ds(pl.multiple_of(c * 512, 512), 512)
        half[:, at] = dot(hot_gather[...], table[:, at]).astype(BF)

    tower_load.wait()

    @pl.loop(0, 2)
    def _(c):
        at = pl.ds(pl.multiple_of(c * 512, 512), 512)
        pre = dot(half[...], w_tower[:, at])
        events[:, at] = (pre * sigmoid(pre)).astype(BF)

    out_load.start()
    grad_load.start()

    @pl.loop(0, 4, unroll=1)
    def _(i):
        at = pl.ds(pl.multiple_of(i * 128, 128), 128)
        x = events[at, :].astype(F32)
        r = lax.rsqrt(jnp.mean(x * x, axis=-1, keepdims=True) + 1e-06)
        inv_rms[at, :] = jnp.broadcast_to(r, (128, 128))
        normed[at, :] = (x * r).astype(BF)

    def product(c, into):
        into[...] = dot(normed[...], w_in[:, pl.ds(pl.multiple_of(c * 512, 512), 512)])

    def activate(c, source):
        at = pl.ds(pl.multiple_of(c * 512, 512), 512)
        pre = source[...]
        sigma = sigmoid(pre)
        act = pre * sigma
        hidden[:, at] = act.astype(BF)
        slope[:, at] = (sigma + act * (1.0 - sigma)).astype(BF)

    for c in in_loads:
        c.wait()
    product(0, pre_a)

    @pl.loop(0, 3)
    def _(i):
        product(2 * i + 1, pre_b)
        activate(2 * i, pre_a)
        product(2 * i + 2, pre_a)
        activate(2 * i + 1, pre_b)

    product(7, pre_b)
    activate(6, pre_a)
    activate(7, pre_b)

    scale = 128 ** (-0.5)
    out_load.wait()
    grad_load.wait()

    @pl.loop(0, HEADS // 2)
    def _(i):
        jobs = [(2 * i + k, b, slice(b * SEQ, (b + 1) * SEQ)) for k in range(2) for b in range(2)]
        head = lambda h, base: pl.ds(pl.multiple_of(base + h * 128, 128), 128)
        score = lambda h, b, rows: dot_nt(
            hidden[rows, head(h, 2 * D)], hidden[rows, head(h, 3 * D)]
        )
        raw = score(*jobs[0])
        for j, (h, b, rows) in enumerate(jobs):
            later = score(*jobs[j + 1]) if j < 3 else None
            turn = jnp.tanh(raw * (0.5 * scale))
            share = coef[b]
            part = share + share * turn
            weights = raw * part
            attn[h, b] = weights.astype(BF)
            rest = (0.5 * scale) - (0.5 * scale) * turn
            attn_slope[h, b] = (part + weights * rest).astype(BF)
            raw = later
        for h, b, rows in jobs:
            mixed[rows, head(h, 0)] = dot(attn[h, b], hidden[rows, head(h, D)])
        at = pl.ds(pl.multiple_of(i * 256, 256), 256)
        dgated[:, at] = dot_nt(grad[...], w_out[at, :]).astype(BF)

    @pl.loop(0, 8, unroll=2)
    def _(i):
        at = pl.ds(pl.multiple_of(i * 64, 64), 64)
        m = mixed[at, :]
        centred = m - jnp.mean(m, axis=-1, keepdims=True)
        r = lax.rsqrt(jnp.mean(centred * centred, axis=-1, keepdims=True) + 1e-05)
        normal = centred * r
        gate = hidden[at, 0:D].astype(F32)
        half[at, :] = (normal * gate).astype(BF)
        dg = dgated[at, :].astype(F32)
        dpre[at, 0:D] = (dg * normal).astype(BF) * slope[at, 0:D]
        dnormal = dg * gate
        m1 = jnp.mean(dnormal, axis=-1, keepdims=True)
        m2 = jnp.mean(dnormal * normal, axis=-1, keepdims=True)
        dmixed[at, :] = (r * (dnormal - m1 - normal * m2)).astype(BF)

    @pl.loop(0, HEADS // 2)
    def _(i):
        jobs = [(2 * i + k, b, slice(b * SEQ, (b + 1) * SEQ)) for k in range(2) for b in range(2)]
        head = lambda h, base: pl.ds(pl.multiple_of(base + h * 128, 128), 128)

        def put(h, rows, base, d):
            dpre[rows, head(h, base)] = d.astype(BF) * slope[rows, head(h, base)]

        dws = [dot_nt(dmixed[rows, head(h, 0)], hidden[rows, head(h, D)]) for h, b, rows in jobs]
        dss = [
            dw.astype(BF) * attn_slope[h, b]
            for dw, (h, b, rows) in zip(dws, jobs)
        ]
        for h, b, rows in jobs:
            put(h, rows, D, dot_tn(attn[h, b], dmixed[rows, head(h, 0)]))
        for ds, (h, b, rows) in zip(dss, jobs):
            put(h, rows, 2 * D, dot(ds, hidden[rows, head(h, 3 * D)]))
            put(h, rows, 3 * D, dot_tn(ds, hidden[rows, head(h, 2 * D)]))
        at = pl.ds(pl.multiple_of(i * 256, 256), 256)
        out_buf[:, at] = (events[:, at].astype(F32) + dot(half[...], w_out[:, at])).astype(BF)

    store = pltpu.make_async_copy(out_buf, events_out_h, sem_out)
    store.start()

    @pl.loop(0, 2)
    def _(c):
        at = pl.ds(pl.multiple_of(c * 512, 512), 512)
        normed[:, at] = dot_nt(dpre[...], w_in[at, :]).astype(BF)

    @pl.loop(0, 4, unroll=1)
    def _(i):
        at = pl.ds(pl.multiple_of(i * 128, 128), 128)
        dn = normed[at, :].astype(F32)
        r = inv_rms[at, 0:1]
        unit = events[at, :].astype(F32) * r
        dx = r * (dn - unit * jnp.mean(dn * unit, axis=-1, keepdims=True))
        half[at, :] = (grad[at, :].astype(F32) + dx).astype(BF)

    z, core = me // 2, me % 2
    keeps, sends = (k0, k1, k2, k3), (s0, s1, s2, s3)
    for k in range(4):
        at = pl.ds(pl.multiple_of((z ^ k) * 256, 256), 256)
        got = dot(hot_scatter[...], half[:, at])
        even, odd = got[:, :128], got[:, 128:]
        keeps[k][...] = jnp.where(core == 0, even, odd).astype(BF)
        sends[k][...] = jnp.where(core == 0, odd, even).astype(BF)
    store.wait()


def layer(pos, lengths, inverse, pieces, w_tower, w_in, w_out, out_grad):
    block = jax.ShapeDtypeStruct((SLOTS, 128), BF)
    vm = pltpu.VMEM
    return pl.pallas_call(
        layer_kernel,
        out_shape=[jax.ShapeDtypeStruct((ROWS, D), BF)] + [block] * 8,
        in_specs=[SMEM, SMEM] + [VMEM] * 9 + [ANY] * 4,
        out_specs=[ANY] + [VMEM] * 8,
        scratch_shapes=[
            vm((SLOTS, D), BF), vm((D, D), BF), vm((D, 4 * D), BF), vm((D, D), BF), vm((ROWS, D), BF),
            vm((ROWS, D), BF), vm((ROWS, D), BF), vm((ROWS, D), BF), vm((ROWS, 4 * D), BF),
            vm((ROWS, 4 * D), BF), vm((HEADS, 2, SEQ, SEQ), BF), vm((HEADS, 2, SEQ, SEQ), BF),
            vm((ROWS, D), F32), vm((ROWS, D), BF), vm((ROWS, D), BF), vm((ROWS, D), BF), vm((ROWS, 4 * D), BF),
            vm((2, SEQ, SEQ), F32), vm((ROWS, 128), F32),
            vm((ROWS, SLOTS), BF), vm((SLOTS, ROWS), BF),
            vm((ROWS, 512), F32), vm((ROWS, 512), F32),
            pltpu.SemaphoreType.DMA((3,)), pltpu.SemaphoreType.DMA((4,)), pltpu.SemaphoreType.DMA,
        ],
        compiler_params=pltpu.CompilerParams(vmem_limit_bytes=50 * MIB),
        cost_estimate=pl.CostEstimate(
            flops=14 * 10**9, bytes_accessed=18 * MIB, transcendentals=4 * MIB
        ),
    )(pos, lengths, inverse, *pieces, w_tower, w_in, w_out, out_grad)


def rows_kernel(pos, p0, p1, p2, p3, p4, p5, p6, p7, w_tower_h, turned, slope, w_cols, sem):
    me = pos[0]
    load = pltpu.make_async_copy(
        w_tower_h.at[:, pl.ds(pl.multiple_of(me * 128, 128), 128)], w_cols, sem
    )
    load.start()
    load.wait()
    for s, piece in enumerate((p0, p1, p2, p3, p4, p5, p6, p7)):
        at = pl.ds(pl.multiple_of((me ^ s) * 128, 128), 128)
        rows = piece[...]
        pre = dot(rows, w_cols[...])
        slope[at, :] = slope_of(pre, sigmoid(pre))
        turned[:, at] = jnp.transpose(rows)


def rows_of(pos, pieces, w_tower):
    return pl.pallas_call(
        rows_kernel,
        out_shape=[jax.ShapeDtypeStruct((D, SLOTS), BF), jax.ShapeDtypeStruct((SLOTS, 128), F32)],
        in_specs=[SMEM] + [VMEM] * 8 + [ANY],
        out_specs=[VMEM, VMEM],
        scratch_shapes=[pltpu.VMEM((D, 128), BF), pltpu.SemaphoreType.DMA],
        compiler_params=pltpu.CompilerParams(vmem_limit_bytes=16 * MIB),
        cost_estimate=pl.CostEstimate(
            flops=2 * SLOTS * D * 128, bytes_accessed=5 * MIB, transcendentals=SLOTS * 128
        ),
    )(pos, *pieces, w_tower)


def slots_kernel(a0, a1, a2, a3, slope, turned, out):
    total = a0[...].astype(F32) + a1[...].astype(F32) + a2[...].astype(F32) + a3[...].astype(F32)
    pre = (total * slope[...]).astype(BF)
    tower = dot(turned[...], pre).reshape(NODES, LOCALS, 8, 128)
    for l in range(LOCALS):
        mine = pre[l * 128 : (l + 1) * 128].astype(F32).reshape(NODES, 8, 128)
        both = jnp.concatenate([mine, tower[:, l]], axis=1)
        out[:, l] = both.astype(BF)


def slots(a, slope, turned):
    return pl.pallas_call(
        slots_kernel,
        out_shape=jax.ShapeDtypeStruct((NODES, LOCALS, 16, 128), BF),
        in_specs=[VMEM] * 6,
        out_specs=VMEM,
        compiler_params=pltpu.CompilerParams(vmem_limit_bytes=16 * MIB),
        cost_estimate=pl.CostEstimate(
            flops=2 * SLOTS * D * 128, bytes_accessed=5 * MIB, transcendentals=0
        ),
    )(*a, slope, turned)


def total_kernel(arrived, out):
    acc = arrived[0, :, :, :].astype(F32)
    for n in range(1, NODES):
        acc = acc + arrived[n, :, :, :].astype(F32)
    row = jnp.concatenate([acc[j, 8:, :] for j in range(LOCALS)], axis=1).astype(BF)
    for n in range(NODES):
        out[n] = row


def total(arrived):
    return pl.pallas_call(
        total_kernel,
        out_shape=jax.ShapeDtypeStruct((NODES, 8, D), BF),
        in_specs=[VMEM],
        out_specs=VMEM,
        compiler_params=pltpu.CompilerParams(vmem_limit_bytes=8 * MIB),
        cost_estimate=pl.CostEstimate(flops=MIB, bytes_accessed=MIB, transcendentals=0),
    )(arrived)


def content_kernel(wanted, arrived, w_tower, tower_rows, out, handed, pre):
    handed[...] = tower_rows[...]
    for n in range(NODES):
        pre[n * 8 : (n + 1) * 8, :] = jnp.concatenate(
            [arrived[n, j].astype(F32)[:8] for j in range(LOCALS)], axis=1
        )
    rows = dot_nt(pre[...].astype(BF), w_tower[...])
    high = rows.astype(BF)
    low = (rows - high.astype(F32)).astype(BF)
    ids = jnp.transpose(wanted[...].reshape(128, 128))
    sub = lax.broadcasted_iota(jnp.int32, (128, 128), 0)
    for j in range(8):
        hot = jnp.where(ids == sub + j * 128, 1.0, 0.0).astype(BF)
        out[j * 128 : (j + 1) * 128, :] = (dot(hot, high) + dot(hot, low)).astype(BF)


def content_side(wanted, arrived, w_tower, tower_rows):
    return pl.pallas_call(
        content_kernel,
        out_shape=[
            jax.ShapeDtypeStruct((1024, D), BF), jax.ShapeDtypeStruct((NODES, 8, D), BF)
        ],
        in_specs=[VMEM] * 4,
        out_specs=[VMEM, VMEM],
        scratch_shapes=[pltpu.VMEM((128, D), F32)],
        compiler_params=pltpu.CompilerParams(vmem_limit_bytes=16 * MIB),
        cost_estimate=pl.CostEstimate(
            flops=6 * 128 * D * D, bytes_accessed=5 * MIB, transcendentals=0
        ),
    )(wanted, arrived, w_tower, tower_rows)


def tower_kernel(which, pos, *refs):
    pieces, out, buf, sem = refs[:4], refs[-3], refs[-2], refs[-1]
    me = pos[0]
    copies = []
    for i, (s, piece) in enumerate(zip(which, pieces)):
        buf[i] = piece[...].astype(F32)
        copies.append(pltpu.make_async_copy(buf.at[i], out.at[:, me ^ s], sem.at[i]))
        copies[-1].start()
    for c in copies:
        c.wait()


def tower_side(which, pos, pieces, *begun):
    return pl.pallas_call(
        functools.partial(tower_kernel, which),
        out_shape=jax.ShapeDtypeStruct((NODES, LOCALS, 8, D), F32),
        in_specs=[SMEM] + [VMEM] * 4 + [ANY] * len(begun),
        out_specs=ANY,
        scratch_shapes=[pltpu.VMEM((4, NODES, 8, D), F32), pltpu.SemaphoreType.DMA((4,))],
        input_output_aliases={5: 0} if begun else {},
        compiler_params=pltpu.CompilerParams(vmem_limit_bytes=16 * MIB),
        cost_estimate=pl.CostEstimate(flops=MIB, bytes_accessed=3 * MIB, transcendentals=0),
    )(pos, *[pieces[s] for s in which], *begun)


def swap(x, s):
    return lax.ppermute(x, "local", [(i, i ^ s) for i in range(LOCALS)])


def gather_local(x, again=None):
    got = {0: x}
    for s in (4, 2, 6):
        got[s] = swap(x, s)
    if again is not None:
        got[0] = again
    for s in (0, 4, 2, 6):
        got[s + 1] = swap(got[s], 1)
    return [got[s] for s in range(LOCALS)]


def body(inverse, slot_rows, lengths, content, w_tower, w_in, w_out, out_grad):
    pos = lax.axis_index("local").astype(jnp.int32).reshape(1)
    asked = ask(slot_rows.reshape(NODES, 8).T)
    wanted = lax.all_to_all(asked, "node", 0, 0, tiled=True)
    picked = pick(wanted, content)
    fetched = lax.all_to_all(picked, "node", 0, 0, tiled=True).reshape(128, D)
    pieces = gather_local(fetched)
    events_out, *blocks = layer(
        pos, lengths, inverse, pieces, w_tower, w_in, w_out, out_grad.reshape(ROWS, D)
    )
    keep, send = blocks[:4], blocks[4:]
    turned, slope = rows_of(pos, pieces, w_tower)
    pair = {k: keep[k] + swap(send[k], 1) for k in (2, 1, 3, 0)}
    arrived = [pair[0]] + [swap(pair[k], 2 * k) for k in (2, 1, 3)]
    out = slots(arrived, slope, turned).reshape(NODES * LOCALS, 16, 128)
    back = lax.all_to_all(out, ("node", "local"), 0, 0, tiled=True).reshape(NODES, LOCALS, 16, 128)
    rows = lax.all_to_all(total(back), "node", 0, 0, tiled=True)
    content_grad, handed = content_side(wanted, back, w_tower, rows)
    near = gather_local(rows, handed)
    begun = tower_side((0, 2, 4, 6), pos, near)
    tower_grad = tower_side((1, 3, 5, 7), pos, near, begun).reshape(D, D)
    return (events_out.reshape(2, SEQ, D), content_grad, tower_grad)


def solution(mesh):
    in_specs = (
        P(("node", "local"), None),
        P("node", "local", None, None),
        P(("node", "local")),
        P(("node", "local"), None),
        P(),
        P(),
        P(),
        P(("node", "local"), None, None),
    )
    out_specs = (P(("node", "local"), None, None), P(("node", "local"), None), P())
    return jax.shard_map(body, mesh=mesh, in_specs=in_specs, out_specs=out_specs, check_vma=False)
```

```python
import functools

import jax
import jax.numpy as jnp
from jax import lax
from jax.experimental import pallas as pl
from jax.experimental.pallas import tpu as pltpu
from jax.sharding import PartitionSpec as P

HEADS = 8
BF = jnp.bfloat16
F32 = jnp.float32
NODES = 16
LOCALS = 8
D = 1024
SLOTS = 1024
ROWS = 512
SEQ = 256
MIB = 1 << 20

VMEM = pl.BlockSpec(memory_space=pltpu.VMEM)
SMEM = pl.BlockSpec(memory_space=pltpu.SMEM)
ANY = pl.BlockSpec(memory_space=pl.ANY)


def dot(a, b):
    return jnp.dot(a, b, preferred_element_type=F32)


def dot_nt(a, b):
    return lax.dot_general(a, b, (((1,), (1,)), ((), ())), preferred_element_type=F32)


def dot_tn(a, b):
    return lax.dot_general(a, b, (((0,), (0,)), ((), ())), preferred_element_type=F32)


def sigmoid(v):
    return 0.5 + 0.5 * jnp.tanh(0.5 * v)


def slope_of(v, sigma):
    return sigma * (1.0 + v * (1.0 - sigma))


def ask_kernel(rows, out):
    for n in range(NODES):
        out[n] = jnp.broadcast_to(rows[:, n : n + 1], (8, 128))


def ask(rows):
    return pl.pallas_call(
        ask_kernel,
        out_shape=jax.ShapeDtypeStruct((NODES, 8, 128), jnp.int32),
        in_specs=[VMEM],
        out_specs=VMEM,
        compiler_params=pltpu.CompilerParams(vmem_limit_bytes=2 * MIB),
        cost_estimate=pl.CostEstimate(flops=20 * 10**9, bytes_accessed=MIB, transcendentals=0),
    )(rows)


def pick_kernel(wanted, content, out):
    ids = wanted[...].reshape(128, 128)
    lane = lax.broadcasted_iota(jnp.int32, (128, 128), 1)
    hot = jnp.concatenate(
        [jnp.where(ids == lane + j * 128, 1.0, 0.0).astype(BF) for j in range(8)], axis=1
    )
    out[...] = dot(hot, content[...]).astype(BF).reshape(NODES, 8, D)


def pick(wanted, content):
    return pl.pallas_call(
        pick_kernel,
        out_shape=jax.ShapeDtypeStruct((NODES, 8, D), BF),
        in_specs=[VMEM, VMEM],
        out_specs=VMEM,
        compiler_params=pltpu.CompilerParams(vmem_limit_bytes=12 * MIB),
        cost_estimate=pl.CostEstimate(flops=2 * 128 * D * D, bytes_accessed=3 * MIB, transcendentals=0),
    )(wanted, content)


def layer_kernel(
    pos, lengths, inverse, p0, p1, p2, p3, p4, p5, p6, p7, w_tower_h, w_in_h, w_out_h, grad_h,
    events_out_h, k0, k1, k2, k3, s0, s1, s2, s3,
    table, w_tower, w_in, w_out, grad, out_buf, events, normed, hidden, slope, attn, attn_slope,
    mixed, half, dgated, dmixed, dpre, coef, inv_rms, hot_gather, hot_scatter, pre_a, pre_b,
    sem_w, sem_in, sem_out,
):
    me = pos[0]
    tower_load = pltpu.make_async_copy(w_tower_h, w_tower, sem_w.at[0])
    out_load = pltpu.make_async_copy(w_out_h, w_out, sem_w.at[1])
    grad_load = pltpu.make_async_copy(grad_h, grad, sem_w.at[2])
    in_loads = [
        pltpu.make_async_copy(
            w_in_h.at[:, pl.ds(j * D, D)], w_in.at[:, pl.ds(j * D, D)], sem_in.at[j]
        )
        for j in range(4)
    ]
    tower_load.start()
    for c in in_loads:
        c.start()
    for s, piece in enumerate((p0, p1, p2, p3, p4, p5, p6, p7)):
        table[pl.ds(pl.multiple_of((me ^ s) * 128, 128), 128), :] = piece[...]

    for b in range(2):
        row = inverse[b : b + 1, :]
        column = jnp.transpose(jnp.broadcast_to(row, (128, SEQ)))
        lane = lax.broadcasted_iota(jnp.int32, (SEQ, 128), 1)
        sub = lax.broadcasted_iota(jnp.int32, (128, SEQ), 0)
        for j in range(8):
            hot_gather[b * SEQ : (b + 1) * SEQ, j * 128 : (j + 1) * 128] = jnp.where(
                column == lane + j * 128, 1.0, 0.0
            ).astype(BF)
            hot_scatter[j * 128 : (j + 1) * 128, b * SEQ : (b + 1) * SEQ] = jnp.where(
                row == sub + j * 128, 1.0, 0.0
            ).astype(BF)
        length = lengths[b]
        query = lax.broadcasted_iota(jnp.int32, (SEQ, SEQ), 0)
        key = lax.broadcasted_iota(jnp.int32, (SEQ, SEQ), 1)
        share = (0.5 * 128 ** (-0.5)) / jnp.full((SEQ, SEQ), length, jnp.int32).astype(F32)
        coef[b] = jnp.where((key <= query) & (query < length), share, 0.0)

    @pl.loop(0, 2)
    def _(c):
        at = pl.ds(pl.multiple_of(c * 512, 512), 512)
        half[:, at] = dot(hot_gather[...], table[:, at]).astype(BF)

    tower_load.wait()

    @pl.loop(0, 2)
    def _(c):
        at = pl.ds(pl.multiple_of(c * 512, 512), 512)
        pre = dot(half[...], w_tower[:, at])
        events[:, at] = (pre * sigmoid(pre)).astype(BF)

    out_load.start()
    grad_load.start()

    @pl.loop(0, 4, unroll=1)
    def _(i):
        at = pl.ds(pl.multiple_of(i * 128, 128), 128)
        x = events[at, :].astype(F32)
        r = lax.rsqrt(jnp.mean(x * x, axis=-1, keepdims=True) + 1e-06)
        inv_rms[at, :] = jnp.broadcast_to(r, (128, 128))
        normed[at, :] = (x * r).astype(BF)

    def product(c, into):
        into[...] = dot(normed[...], w_in[:, pl.ds(pl.multiple_of(c * 512, 512), 512)])

    def activate(c, source):
        at = pl.ds(pl.multiple_of(c * 512, 512), 512)
        pre = source[...]
        sigma = sigmoid(pre)
        act = pre * sigma
        hidden[:, at] = act.astype(BF)
        slope[:, at] = (sigma + act * (1.0 - sigma)).astype(BF)

    for c in in_loads:
        c.wait()
    product(0, pre_a)

    @pl.loop(0, 3)
    def _(i):
        product(2 * i + 1, pre_b)
        activate(2 * i, pre_a)
        product(2 * i + 2, pre_a)
        activate(2 * i + 1, pre_b)

    product(7, pre_b)
    activate(6, pre_a)
    activate(7, pre_b)

    scale = 128 ** (-0.5)
    out_load.wait()
    grad_load.wait()

    @pl.loop(0, HEADS // 2)
    def _(i):
        jobs = [(2 * i + k, b, slice(b * SEQ, (b + 1) * SEQ)) for k in range(2) for b in range(2)]
        head = lambda h, base: pl.ds(pl.multiple_of(base + h * 128, 128), 128)
        score = lambda h, b, rows: dot_nt(
            hidden[rows, head(h, 2 * D)], hidden[rows, head(h, 3 * D)]
        )
        raw = score(*jobs[0])
        for j, (h, b, rows) in enumerate(jobs):
            later = score(*jobs[j + 1]) if j < 3 else None
            turn = jnp.tanh(raw * (0.5 * scale))
            share = coef[b]
            part = share + share * turn
            weights = raw * part
            attn[h, b] = weights.astype(BF)
            rest = (0.5 * scale) - (0.5 * scale) * turn
            attn_slope[h, b] = (part + weights * rest).astype(BF)
            raw = later
        for h, b, rows in jobs:
            mixed[rows, head(h, 0)] = dot(attn[h, b], hidden[rows, head(h, D)])
        at = pl.ds(pl.multiple_of(i * 256, 256), 256)
        dgated[:, at] = dot_nt(grad[...], w_out[at, :]).astype(BF)

    @pl.loop(0, 8, unroll=2)
    def _(i):
        at = pl.ds(pl.multiple_of(i * 64, 64), 64)
        m = mixed[at, :]
        centred = m - jnp.mean(m, axis=-1, keepdims=True)
        r = lax.rsqrt(jnp.mean(centred * centred, axis=-1, keepdims=True) + 1e-05)
        normal = centred * r
        gate = hidden[at, 0:D].astype(F32)
        half[at, :] = (normal * gate).astype(BF)
        dg = dgated[at, :].astype(F32)
        dpre[at, 0:D] = (dg * normal).astype(BF) * slope[at, 0:D]
        dnormal = dg * gate
        m1 = jnp.mean(dnormal, axis=-1, keepdims=True)
        m2 = jnp.mean(dnormal * normal, axis=-1, keepdims=True)
        dmixed[at, :] = (r * (dnormal - m1 - normal * m2)).astype(BF)

    @pl.loop(0, HEADS // 2)
    def _(i):
        jobs = [(2 * i + k, b, slice(b * SEQ, (b + 1) * SEQ)) for k in range(2) for b in range(2)]
        head = lambda h, base: pl.ds(pl.multiple_of(base + h * 128, 128), 128)

        def put(h, rows, base, d):
            dpre[rows, head(h, base)] = d.astype(BF) * slope[rows, head(h, base)]

        dws = [dot_nt(dmixed[rows, head(h, 0)], hidden[rows, head(h, D)]) for h, b, rows in jobs]
        dss = [
            dw.astype(BF) * attn_slope[h, b]
            for dw, (h, b, rows) in zip(dws, jobs)
        ]
        for h, b, rows in jobs:
            put(h, rows, D, dot_tn(attn[h, b], dmixed[rows, head(h, 0)]))
        for ds, (h, b, rows) in zip(dss, jobs):
            put(h, rows, 2 * D, dot(ds, hidden[rows, head(h, 3 * D)]))
            put(h, rows, 3 * D, dot_tn(ds, hidden[rows, head(h, 2 * D)]))
        at = pl.ds(pl.multiple_of(i * 256, 256), 256)
        out_buf[:, at] = (events[:, at].astype(F32) + dot(half[...], w_out[:, at])).astype(BF)

    store = pltpu.make_async_copy(out_buf, events_out_h, sem_out)
    store.start()

    @pl.loop(0, 2)
    def _(c):
        at = pl.ds(pl.multiple_of(c * 512, 512), 512)
        normed[:, at] = dot_nt(dpre[...], w_in[at, :]).astype(BF)

    @pl.loop(0, 4, unroll=1)
    def _(i):
        at = pl.ds(pl.multiple_of(i * 128, 128), 128)
        dn = normed[at, :].astype(F32)
        r = inv_rms[at, 0:1]
        unit = events[at, :].astype(F32) * r
        dx = r * (dn - unit * jnp.mean(dn * unit, axis=-1, keepdims=True))
        half[at, :] = (grad[at, :].astype(F32) + dx).astype(BF)

    z, core = me // 2, me % 2
    keeps, sends = (k0, k1, k2, k3), (s0, s1, s2, s3)
    for k in range(4):
        at = pl.ds(pl.multiple_of((z ^ k) * 256, 256), 256)
        got = dot(hot_scatter[...], half[:, at])
        even, odd = got[:, :128], got[:, 128:]
        keeps[k][...] = jnp.where(core == 0, even, odd).astype(BF)
        sends[k][...] = jnp.where(core == 0, odd, even).astype(BF)
    store.wait()


def layer(pos, lengths, inverse, pieces, w_tower, w_in, w_out, out_grad):
    block = jax.ShapeDtypeStruct((SLOTS, 128), BF)
    vm = pltpu.VMEM
    return pl.pallas_call(
        layer_kernel,
        out_shape=[jax.ShapeDtypeStruct((ROWS, D), BF)] + [block] * 8,
        in_specs=[SMEM, SMEM] + [VMEM] * 9 + [ANY] * 4,
        out_specs=[ANY] + [VMEM] * 8,
        scratch_shapes=[
            vm((SLOTS, D), BF), vm((D, D), BF), vm((D, 4 * D), BF), vm((D, D), BF), vm((ROWS, D), BF),
            vm((ROWS, D), BF), vm((ROWS, D), BF), vm((ROWS, D), BF), vm((ROWS, 4 * D), BF),
            vm((ROWS, 4 * D), BF), vm((HEADS, 2, SEQ, SEQ), BF), vm((HEADS, 2, SEQ, SEQ), BF),
            vm((ROWS, D), F32), vm((ROWS, D), BF), vm((ROWS, D), BF), vm((ROWS, D), BF), vm((ROWS, 4 * D), BF),
            vm((2, SEQ, SEQ), F32), vm((ROWS, 128), F32),
            vm((ROWS, SLOTS), BF), vm((SLOTS, ROWS), BF),
            vm((ROWS, 512), F32), vm((ROWS, 512), F32),
            pltpu.SemaphoreType.DMA((3,)), pltpu.SemaphoreType.DMA((4,)), pltpu.SemaphoreType.DMA,
        ],
        compiler_params=pltpu.CompilerParams(vmem_limit_bytes=50 * MIB),
        cost_estimate=pl.CostEstimate(
            flops=14 * 10**9, bytes_accessed=18 * MIB, transcendentals=4 * MIB
        ),
    )(pos, lengths, inverse, *pieces, w_tower, w_in, w_out, out_grad)


def rows_kernel(pos, p0, p1, p2, p3, p4, p5, p6, p7, w_tower_h, turned, slope, w_cols, sem):
    me = pos[0]
    load = pltpu.make_async_copy(
        w_tower_h.at[:, pl.ds(pl.multiple_of(me * 128, 128), 128)], w_cols, sem
    )
    load.start()
    load.wait()
    for s, piece in enumerate((p0, p1, p2, p3, p4, p5, p6, p7)):
        at = pl.ds(pl.multiple_of((me ^ s) * 128, 128), 128)
        rows = piece[...]
        pre = dot(rows, w_cols[...])
        slope[at, :] = slope_of(pre, sigmoid(pre))
        turned[:, at] = jnp.transpose(rows)


def rows_of(pos, pieces, w_tower):
    return pl.pallas_call(
        rows_kernel,
        out_shape=[jax.ShapeDtypeStruct((D, SLOTS), BF), jax.ShapeDtypeStruct((SLOTS, 128), F32)],
        in_specs=[SMEM] + [VMEM] * 8 + [ANY],
        out_specs=[VMEM, VMEM],
        scratch_shapes=[pltpu.VMEM((D, 128), BF), pltpu.SemaphoreType.DMA],
        compiler_params=pltpu.CompilerParams(vmem_limit_bytes=16 * MIB),
        cost_estimate=pl.CostEstimate(
            flops=2 * SLOTS * D * 128, bytes_accessed=5 * MIB, transcendentals=SLOTS * 128
        ),
    )(pos, *pieces, w_tower)


def slots_kernel(a0, a1, a2, a3, slope, turned, out):
    total = a0[...].astype(F32) + a1[...].astype(F32) + a2[...].astype(F32) + a3[...].astype(F32)
    pre = (total * slope[...]).astype(BF)
    tower = dot(turned[...], pre).reshape(NODES, LOCALS, 8, 128)
    for l in range(LOCALS):
        mine = pre[l * 128 : (l + 1) * 128].astype(F32).reshape(NODES, 8, 128)
        both = jnp.concatenate([mine, tower[:, l]], axis=1)
        out[:, l] = both.astype(BF)


def slots(a, slope, turned):
    return pl.pallas_call(
        slots_kernel,
        out_shape=jax.ShapeDtypeStruct((NODES, LOCALS, 16, 128), BF),
        in_specs=[VMEM] * 6,
        out_specs=VMEM,
        compiler_params=pltpu.CompilerParams(vmem_limit_bytes=16 * MIB),
        cost_estimate=pl.CostEstimate(
            flops=2 * SLOTS * D * 128, bytes_accessed=5 * MIB, transcendentals=0
        ),
    )(*a, slope, turned)


def total_kernel(arrived, out):
    acc = arrived[0, :, :, :].astype(F32)
    for n in range(1, NODES):
        acc = acc + arrived[n, :, :, :].astype(F32)
    row = jnp.concatenate([acc[j, 8:, :] for j in range(LOCALS)], axis=1).astype(BF)
    for n in range(NODES):
        out[n] = row


def total(arrived):
    return pl.pallas_call(
        total_kernel,
        out_shape=jax.ShapeDtypeStruct((NODES, 8, D), BF),
        in_specs=[VMEM],
        out_specs=VMEM,
        compiler_params=pltpu.CompilerParams(vmem_limit_bytes=8 * MIB),
        cost_estimate=pl.CostEstimate(flops=MIB, bytes_accessed=MIB, transcendentals=0),
    )(arrived)


def content_kernel(wanted, arrived, w_tower, tower_rows, out, handed, pre):
    handed[...] = tower_rows[...]
    for n in range(NODES):
        pre[n * 8 : (n + 1) * 8, :] = jnp.concatenate(
            [arrived[n, j].astype(F32)[:8] for j in range(LOCALS)], axis=1
        )
    rows = dot_nt(pre[...].astype(BF), w_tower[...])
    high = rows.astype(BF)
    low = (rows - high.astype(F32)).astype(BF)
    ids = jnp.transpose(wanted[...].reshape(128, 128))
    sub = lax.broadcasted_iota(jnp.int32, (128, 128), 0)
    for j in range(8):
        hot = jnp.where(ids == sub + j * 128, 1.0, 0.0).astype(BF)
        out[j * 128 : (j + 1) * 128, :] = (dot(hot, high) + dot(hot, low)).astype(BF)


def content_side(wanted, arrived, w_tower, tower_rows):
    return pl.pallas_call(
        content_kernel,
        out_shape=[
            jax.ShapeDtypeStruct((1024, D), BF), jax.ShapeDtypeStruct((NODES, 8, D), BF)
        ],
        in_specs=[VMEM] * 4,
        out_specs=[VMEM, VMEM],
        scratch_shapes=[pltpu.VMEM((128, D), F32)],
        compiler_params=pltpu.CompilerParams(vmem_limit_bytes=16 * MIB),
        cost_estimate=pl.CostEstimate(
            flops=6 * 128 * D * D, bytes_accessed=5 * MIB, transcendentals=0
        ),
    )(wanted, arrived, w_tower, tower_rows)


def tower_kernel(which, pos, *refs):
    pieces, out, buf, sem = refs[: len(which)], refs[-3], refs[-2], refs[-1]
    me = pos[0]
    copies = []
    for i, (s, piece) in enumerate(zip(which, pieces)):
        buf[i] = piece[...].astype(F32)
        copies.append(pltpu.make_async_copy(buf.at[i], out.at[:, me ^ s], sem.at[i]))
        copies[-1].start()
    for c in copies:
        c.wait()


def tower_side(which, pos, pieces, *begun):
    return pl.pallas_call(
        functools.partial(tower_kernel, which),
        out_shape=jax.ShapeDtypeStruct((NODES, LOCALS, 8, D), F32),
        in_specs=[SMEM] + [VMEM] * len(which) + [ANY] * len(begun),
        out_specs=ANY,
        scratch_shapes=[pltpu.VMEM((5, NODES, 8, D), F32), pltpu.SemaphoreType.DMA((5,))],
        input_output_aliases={1 + len(which): 0} if begun else {},
        compiler_params=pltpu.CompilerParams(vmem_limit_bytes=16 * MIB),
        cost_estimate=pl.CostEstimate(flops=MIB, bytes_accessed=3 * MIB, transcendentals=0),
    )(pos, *[pieces[s] for s in which], *begun)


def swap(x, s):
    return lax.ppermute(x, "local", [(i, i ^ s) for i in range(LOCALS)])


def gather_local(x, again=None):
    got = {0: x}
    for s in (4, 2, 6):
        got[s] = swap(x, s)
    if again is not None:
        got[0] = again
    for s in (0, 4, 2, 6):
        got[s + 1] = swap(got[s], 1)
    return [got[s] for s in range(LOCALS)]


def body(inverse, slot_rows, lengths, content, w_tower, w_in, w_out, out_grad):
    pos = lax.axis_index("local").astype(jnp.int32).reshape(1)
    asked = ask(slot_rows.reshape(NODES, 8).T)
    wanted = lax.all_to_all(asked, "node", 0, 0, tiled=True)
    picked = pick(wanted, content)
    fetched = lax.all_to_all(picked, "node", 0, 0, tiled=True).reshape(128, D)
    pieces = gather_local(fetched)
    events_out, *blocks = layer(
        pos, lengths, inverse, pieces, w_tower, w_in, w_out, out_grad.reshape(ROWS, D)
    )
    keep, send = blocks[:4], blocks[4:]
    turned, slope = rows_of(pos, pieces, w_tower)
    pair = {k: keep[k] + swap(send[k], 1) for k in (2, 1, 3, 0)}
    arrived = [pair[0]] + [swap(pair[k], 2 * k) for k in (2, 1, 3)]
    out = slots(arrived, slope, turned).reshape(NODES * LOCALS, 16, 128)
    back = lax.all_to_all(out, ("node", "local"), 0, 0, tiled=True).reshape(NODES, LOCALS, 16, 128)
    rows = lax.all_to_all(total(back), "node", 0, 0, tiled=True)
    content_grad, handed = content_side(wanted, back, w_tower, rows)
    near = gather_local(rows, handed)
    begun = tower_side((0, 1, 2, 4, 6), pos, near)
    tower_grad = tower_side((3, 5, 7), pos, near, begun).reshape(D, D)
    return (events_out.reshape(2, SEQ, D), content_grad, tower_grad)


def solution(mesh):
    in_specs = (
        P(("node", "local"), None),
        P("node", "local", None, None),
        P(("node", "local")),
        P(("node", "local"), None),
        P(),
        P(),
        P(),
        P(("node", "local"), None, None),
    )
    out_specs = (P(("node", "local"), None, None), P(("node", "local"), None), P())
    return jax.shard_map(body, mesh=mesh, in_specs=in_specs, out_specs=out_specs, check_vma=False)
```
